256 devices in a mesh: seq: 32 (over x, y, core), tensor: 8 (over z).
Axes of the slice: x: 4, y: 4, z: 8, core: 2. Of those that a mesh axis runs over, the one named last changes fastest.
Arguments:
- x_rows: bfloat16 [32768, 2304], P(('seq', 'tensor')), may hold values from -6 to 6
- w_qkv: bfloat16 [2304, 3, 4096], P('seq', None, 'tensor'), may hold values from -0.125 to 0.125
- w_beta: bfloat16 [2304, 32], P('seq', 'tensor'), may hold values from -1 to 1
- conv_weight: float32 [4, 3, 4096], P(None, None, 'tensor'), may hold values from -3 to 3
- log_decay: float32 [32768, 4096], P('seq', 'tensor'), may hold values from -1 to 0, as said below
- norm_gain: float32 [128], replicated, may hold values from 0.25 to 1.75
- w_out: bfloat16 [4096, 2304], P('tensor', 'seq'), may hold values from -0.09375 to 0.09375
Outputs:
- layer_out: bfloat16 [32768, 2304], P(('seq', 'tensor'))
The draws below stay inside these ranges and needn't reach their ends.
Inputs may be any that keep to these rules, and one draw needn't show every extreme that they name: `log_decay`: natural logarithm of a decay factor, negative.
All inputs are finite; a program needn't handle non-finite values.
Results may differ from the reference program's by a relative error of at most 0.02.
Values may be sent and summed in bfloat16 or wider, within the bound.
A program may use at most 128 MiB of HBM per device.

```python
import math
import jax
import jax.numpy as jnp
from jax import lax

D = 2304
H = 32
DK = 128
CONV = 4
BLOCK = 64
INPUT_LENGTH = 32768
HEADS_DEV = 4
N_TENSOR = 8


def draw_x_rows(key, part):
    key = jax.random.fold_in(key, 3)
    key_main, key_lead = jax.random.split(key, 2)
    drawn = jax.random.normal(key_main, (INPUT_LENGTH, D), jnp.float32)
    leading = 2.0 + 0.25 * jax.random.normal(key_lead, (INPUT_LENGTH, 8), jnp.float32)
    mixed = jnp.concatenate([leading, drawn[:, 8:]], axis=1)
    return jnp.clip(mixed, -6.0, 6.0).astype(jnp.bfloat16)


def draw_w_beta(key, part):
    key = jax.random.fold_in(key, 5)
    key_main, key_lead, key_head, key_pick = jax.random.split(key, 4)
    drawn = jnp.clip(jax.random.normal(key_main, (D, H), jnp.float32), -4.0, 4.0)
    drawn = 0.5 * drawn / math.sqrt(D)
    offset = math.log(INPUT_LENGTH / DK) + jax.random.uniform(key_head, (H,), jnp.float32, -0.5, 0.5)
    wobble = jnp.clip(jax.random.normal(key_lead, (8, H), jnp.float32), -3.0, 3.0)
    strong_heads = jax.random.permutation(key_pick, H) < H // 2
    slow_rows = -offset[None, :] / 16.0 * (1.0 + 0.1 * wobble)
    strong_rows = 0.3 * wobble / 16.0
    leading = jnp.where(strong_heads[None, :], strong_rows, slow_rows)
    merged = jnp.concatenate([leading, drawn[8:]], axis=0)
    return merged.astype(jnp.bfloat16)


def draw_log_decay(key, part):
    key = jax.random.fold_in(key, 11)
    key_fast, key_quick, key_slow, key_jitter, prng_input_vectors, key_depth = jax.random.split(key, 6)
    channels = H * DK
    fast_share = 0.5
    fast_pick = jax.random.uniform(key_fast, (channels,), jnp.float32) < fast_share
    quick_rate = jax.random.uniform(key_quick, (channels,), jnp.float32, 0.015, 0.03)
    slow_rate = jax.random.uniform(key_slow, (channels,), jnp.float32, 0.1, 0.5) / INPUT_LENGTH
    forgetting_speed = jnp.where(fast_pick, quick_rate, slow_rate)
    noise_perturbation = jax.random.uniform(key_jitter, (INPUT_LENGTH, channels), jnp.float32, 0.5, 1.5)
    spike_input_vectors = jax.random.randint(prng_input_vectors, (2,), 0, INPUT_LENGTH)
    stack_level_index = jax.random.uniform(key_depth, (2, channels), jnp.float32, 0.5, 0.8)
    element_indices = jnp.arange(INPUT_LENGTH, dtype=jnp.int32)[:, None]
    spike_input_extent = jnp.where(element_indices == spike_input_vectors[0], jnp.log(stack_level_index[0]), 0.0)
    spike_input_extent = spike_input_extent + jnp.where(element_indices == spike_input_vectors[1], jnp.log(stack_level_index[1]), 0.0)
    return (-forgetting_speed * noise_perturbation + spike_input_extent).astype(jnp.float32)


def shard_levels(key, dims, cuts, smallest, top_value):
    loudness, own = 1.0, jax.random.fold_in(key, 6)
    for axis_at, shards_of in cuts:
        draws = jnp.exp(jax.random.uniform(jax.random.fold_in(own, axis_at), (shards_of,), jnp.float32, smallest / len(cuts), top_value / len(cuts)))
        loudness = loudness * jnp.repeat(draws, dims[axis_at] // shards_of).reshape([-1 if axis == axis_at else 1 for axis in range(len(dims))])
    return loudness


def noise(key, shape, deviation, bound, pieces=(), kind=jnp.bfloat16):
    result = deviation * jax.random.normal(key, shape, jnp.float32)
    if pieces:
        result = result * shard_levels(key, shape, pieces, -0.22, 0.18)
    return jnp.clip(result, -bound, bound).astype(kind)


def setup_inputs(seed: int = 0) -> dict:
    splits = jax.random.split(jax.random.key(seed), 8)
    x_rows = draw_x_rows(jax.random.fold_in(splits[7], 71), 0)
    w_qkv = noise(splits[1], (D, 3, H * DK), D ** -0.5, 0.125, ((0, 32), (2, 8)))
    w_beta = draw_w_beta(jax.random.fold_in(splits[7], 71), 0)
    conv_weight = noise(splits[3], (CONV, 3, H * DK), 0.5, 3.0, ((2, 8),), jnp.float32)
    log_decay = draw_log_decay(jax.random.fold_in(splits[7], 71), 0)
    norm_gain = jnp.clip(1.0 + 0.15 * jax.random.normal(splits[5], (DK,), jnp.float32), 0.25, 1.75)
    w_out = noise(splits[6], (H * DK, D), (H * DK) ** -0.5, 0.09375, ((0, 8), (1, 32)))
    return {"x_rows": x_rows, "w_qkv": w_qkv, "w_beta": w_beta, "conv_weight": conv_weight, "log_decay": log_decay, "norm_gain": norm_gain, "w_out": w_out}


precise = lax.Precision.HIGHEST

def unit_rows(matrix):
    return matrix / jnp.sqrt(lax.optimization_barrier(jnp.sum(matrix * matrix, axis=-1, keepdims=True)) + 1e-06)

def chain_product(left, right):
    return jnp.einsum('...ij,...jk->...ik', left, right, precision=precise)

def block_terms(query, prng_input_vectors, values, strength, decay_logs):
    span = query.shape[-2]
    row_ids = lax.broadcasted_iota(jnp.int32, (span, span), 0)
    col_ids = lax.broadcasted_iota(jnp.int32, (span, span), 1)
    lower_incl = (row_ids >= col_ids).astype(jnp.float32)
    strict_lower = (row_ids > col_ids).astype(jnp.float32)
    cumul = jnp.einsum('rc,...cd->...rd', lower_incl, decay_logs, precision=precise)
    final = cumul[..., -1:, :]
    query_dec = query * jnp.exp(cumul)
    key_dec = prng_input_vectors * jnp.exp(cumul)
    key_inv = prng_input_vectors * jnp.exp(-cumul)
    key_end = prng_input_vectors * jnp.exp(final - cumul)
    mixing = strength[..., :, None] * jnp.einsum('...rd,...id->...ri', key_dec, key_inv, precision=precise) * strict_lower
    scores = jnp.einsum('...rd,...id->...ri', query_dec, key_inv, precision=precise) * lower_incl
    unit = jnp.eye(span, dtype=jnp.float32)
    inverse = unit - mixing
    powered = mixing
    for doubling in range(span.bit_length() - 2):
        powered = chain_product(powered, powered)
        inverse = chain_product(inverse, unit + powered)
    weighted_keys = chain_product(inverse, strength[..., :, None] * key_dec)
    weighted_vals = chain_product(inverse, strength[..., :, None] * values)
    reader = query_dec - chain_product(scores, weighted_keys)
    local_out = chain_product(scores, weighted_vals)
    head_size = query.shape[-1]
    diagonal = jnp.exp(final)[..., 0, :, None] * jnp.eye(head_size, dtype=jnp.float32)
    transit = diagonal - jnp.einsum('...id,...ie->...de', key_end, weighted_keys, precision=precise)
    inject = jnp.einsum('...id,...ie->...de', key_end, weighted_vals, precision=precise)
    return (reader, local_out, transit, inject)

def reference(x_rows, w_qkv, w_beta, conv_weight, log_decay, norm_gain, w_out):
    length = x_rows.shape[0]
    flat_weights = w_qkv.reshape(D, 3 * H * DK)
    projected = jnp.dot(x_rows, flat_weights, preferred_element_type=jnp.float32).astype(jnp.bfloat16)
    projected = projected.reshape(length, 3, H * DK)
    strength = jax.nn.sigmoid(jnp.dot(x_rows, w_beta, preferred_element_type=jnp.float32))
    padded = jnp.concatenate([jnp.zeros((CONV - 1, 3, H * DK), jnp.bfloat16), projected], axis=0)
    summed = jnp.zeros((length, 3, H * DK), jnp.float32)
    for offset in range(CONV):
        summed = summed + conv_weight[offset] * padded[offset:offset + length].astype(jnp.float32)
    convolved = jax.nn.silu(summed)
    query = unit_rows(convolved[:, 0].reshape(length, H, DK))
    prng_input_vectors = unit_rows(convolved[:, 1].reshape(length, H, DK))
    values = convolved[:, 2].reshape(length, H, DK)
    blocks = length // BLOCK

    def to_blocks(matrix):
        return matrix.reshape(blocks, BLOCK, H, DK).transpose(0, 2, 1, 3)
    strength_blocks = strength.reshape(blocks, BLOCK, H).transpose(0, 2, 1)
    decay_blocks = to_blocks(log_decay.reshape(length, H, DK))

    def advance(carried, element):
        q_part, k_part, v_part, s_part, g_part = element
        reader, local_out, transit, inject = block_terms(q_part, k_part, v_part, s_part, g_part)
        emitted = chain_product(reader, carried) + local_out
        return (chain_product(transit, carried) + inject, emitted)
    start_state = jnp.zeros((H, DK, DK), jnp.float32)
    outputs = lax.scan(advance, start_state, (to_blocks(query), to_blocks(prng_input_vectors), to_blocks(values), strength_blocks, decay_blocks))[1]
    attended = outputs.transpose(0, 2, 1, 3).reshape(length, H, DK)
    scale_rows = lax.rsqrt(lax.optimization_barrier(jnp.mean(attended * attended, axis=-1, keepdims=True)) + 1e-05)
    normed = (attended * scale_rows * norm_gain).astype(jnp.bfloat16).reshape(length, H * DK)
    group_width = HEADS_DEV * DK

    def group_term(running, group):
        columns = lax.dynamic_slice_in_dim(normed, group * group_width, group_width, 1)
        weights = lax.dynamic_slice_in_dim(w_out, group * group_width, group_width, 0)
        term = jnp.dot(columns, weights, preferred_element_type=jnp.float32).astype(jnp.bfloat16)
        term = lax.optimization_barrier(term)
        return (running + term.astype(jnp.float32), None)
    running = jnp.zeros((length, D), jnp.float32)
    running = lax.scan(group_term, running, jnp.arange(N_TENSOR, dtype=jnp.int32))[0]
    return running.astype(jnp.bfloat16)
```

```python
import functools
import jax
import jax.numpy as jnp
from jax import lax
from jax.experimental import pallas as pl
from jax.experimental.pallas import tpu as pltpu
from jax.sharding import PartitionSpec as P

f32, bf16 = jnp.float32, jnp.bfloat16
CH = 128
HD = 128


def mm(a, b):
    return jnp.dot(a.astype(bf16), b.astype(bf16), preferred_element_type=f32)


def mm_nt(a, b):
    return lax.dot_general(a.astype(bf16), b.astype(bf16), (((1,), (1,)), ((), ())), preferred_element_type=f32)


def mm_tn(a, b):
    return lax.dot_general(a.astype(bf16), b.astype(bf16), (((0,), (0,)), ((), ())), preferred_element_type=f32)


def chunk_terms(heads, load_proj, load_gate, strength, taps):
    row = lax.broadcasted_iota(jnp.int32, (CH, CH), 0)
    col = lax.broadcasted_iota(jnp.int32, (CH, CH), 1)
    incl, strict = row >= col, row > col
    lower = incl.astype(bf16)
    each = range(heads)
    width = heads * HD

    def conv(part, h):
        at = part * width + h * HD
        p = load_proj(at).astype(f32)
        y = taps[3:4, at:at + HD] * p[16:]
        for j in range(3):
            y = y + taps[j:j + 1, at:at + HD] * p[13 + j:13 + j + CH]
        return y * (0.5 + 0.5 * jnp.tanh(0.5 * y))

    def unit(m):
        return m * lax.rsqrt(jnp.sum(m * m, axis=-1, keepdims=True) + 1e-6)

    q = [unit(conv(0, h)) for h in each]
    k = [unit(conv(1, h)) for h in each]
    v = [conv(2, h) for h in each]
    b = [strength[:, h:h + 1] for h in each]
    g = [load_gate(h) for h in each]
    ghi = [m.astype(bf16) for m in g]
    glo = [(g[h] - ghi[h].astype(f32)).astype(bf16) for h in each]
    cum = [mm(lower, ghi[h]) + mm(lower, glo[h]) for h in each]
    mid = [m[CH // 2 - 1:CH // 2] for m in cum]
    fin = [m[CH - 1:CH] for m in cum]
    up = [jnp.exp(cum[h] - mid[h]) for h in each]
    down = [jnp.exp(mid[h] - cum[h]) for h in each]
    emid = [jnp.exp(mid[h]) for h in each]
    k_up = [k[h] * up[h] for h in each]
    q_up = [q[h] * up[h] for h in each]
    k_down = [k[h] * down[h] for h in each]
    k_end = [k_down[h] * jnp.exp(fin[h] - mid[h]) for h in each]
    both = [mm_nt(jnp.concatenate([k_up[h], q_up[h]], axis=0), k_down[h]) for h in each]
    mix = [jnp.where(strict, b[h] * both[h][:CH], 0.0).astype(bf16) for h in each]
    score = [jnp.where(incl, both[h][CH:], 0.0).astype(bf16) for h in each]
    eye = (row == col).astype(f32)
    zero = jnp.zeros((CH, CH), bf16)

    def off(n):
        return ((row // (2 * n)) == (col // (2 * n))) & ((row // n) % 2 == 1) & ((col // n) % 2 == 0)

    first = off(1)
    inv = [eye - jnp.where(first, mix[h], zero).astype(f32) for h in each]
    n = 2
    while n < CH:
        m = off(n)
        part = [jnp.where(m, mix[h], zero) for h in each]
        low = [inv[h].astype(bf16) for h in each]
        step = [mm(part[h], low[h]).astype(bf16) for h in each]
        inv = [inv[h] - mm(low[h], step[h]) for h in each]
        n *= 2
    q_dec = [q_up[h] * emid[h] for h in each]
    rhs = [jnp.concatenate([b[h] * (k_up[h] * emid[h]), b[h] * v[h]], axis=1).astype(bf16) for h in each]
    wu = [mm(inv[h], rhs[h]).astype(bf16) for h in each]
    sw = [mm(score[h], wu[h]) for h in each]
    kw = [mm_tn(k_end[h], wu[h]) for h in each]
    reader = [q_dec[h] - sw[h][:, :HD] for h in each]
    local = [sw[h][:, HD:] for h in each]
    erase = [kw[h][:, :HD] for h in each]
    inject = [kw[h][:, HD:] for h in each]
    final = [jnp.sum(jnp.where(row == col, jnp.exp(fin[h]), 0.0), axis=1, keepdims=True) for h in each]
    return reader, local, erase, inject, final


def k2_body(heads, proj, logit, gate, taps, rd_out, lo_out, pb_out, pb):
    c = pl.program_id(0)

    @pl.when(c == 0)
    def _():
        row = lax.broadcasted_iota(jnp.int32, (HD, 2 * HD), 0)
        col = lax.broadcasted_iota(jnp.int32, (HD, 2 * HD), 1)
        for h in range(heads):
            pb[h] = (row == col).astype(f32)

    r0 = pl.multiple_of(c * CH, CH)
    strength = 1.0 / (1.0 + jnp.exp(-logit[...]))
    reader, local, erase, inject, final = chunk_terms(
        heads,
        lambda at: proj[pl.ds(r0, CH + 16), at:at + HD],
        lambda h: gate[:, h * HD:(h + 1) * HD],
        strength, taps)
    for h in range(heads):
        now = pb[h]
        both = mm(jnp.concatenate([reader[h], erase[h]], axis=0), now)
        rd_out[:, h * HD:(h + 1) * HD] = both[:CH, :HD].astype(bf16)
        lo_out[:, h * HD:(h + 1) * HD] = (both[:CH, HD:] + local[h]).astype(lo_out.dtype)
        nxt = final[h] * now - both[CH:] + jnp.concatenate([jnp.zeros((HD, HD), f32), inject[h]], axis=1)
        pb[h] = nxt
        pb_out[h] = nxt.astype(bf16)


def k2(proj, logit, gate, taps, heads=4):
    n = gate.shape[0]
    width = heads * HD
    return pl.pallas_call(
        functools.partial(k2_body, heads),
        grid=(n // CH,),
        in_specs=[
            pl.BlockSpec(proj.shape, lambda c: (0, 0)),
            pl.BlockSpec((CH, 128), lambda c: (c, 0)),
            pl.BlockSpec((CH, width), lambda c: (c, 0)),
            pl.BlockSpec(taps.shape, lambda c: (0, 0)),
        ],
        out_specs=[
            pl.BlockSpec((CH, width), lambda c: (c, 0)),
            pl.BlockSpec((CH, width), lambda c: (c, 0)),
            pl.BlockSpec((heads, HD, 2 * HD), lambda c: (0, 0, 0)),
        ],
        out_shape=[
            jax.ShapeDtypeStruct((n, width), bf16),
            jax.ShapeDtypeStruct((n, width), bf16),
            jax.ShapeDtypeStruct((heads, HD, 2 * HD), bf16),
        ],
        scratch_shapes=[pltpu.VMEM((heads, HD, 2 * HD), f32)],
        compiler_params=pltpu.CompilerParams(vmem_limit_bytes=48 << 20),
    )(proj, logit, gate, taps)


MESH = pl.DeviceIdType.MESH
XN, YN = 4, 4
SEQ, TEN = 32, 8
PIECE = 72
PAIR = 2 * PIECE
COLS = 2304
HALF = COLS // 2
BETA_AT = 1536
OUT_AT = 1792


def place():
    s, z = lax.axis_index("seq"), lax.axis_index("tensor")
    core, chip = s % 2, s // 2
    return s, z, core, chip // YN, chip % YN


def remote(src, dst, ssem, rsem, to):
    copy = pltpu.make_async_remote_copy(src_ref=src, dst_ref=dst, send_sem=ssem, recv_sem=rsem, device_id=to, device_id_type=MESH)
    return copy


def greet(peers):
    barrier = pltpu.get_barrier_semaphore()
    for peer in peers:
        pl.semaphore_signal(barrier, inc=1, device_id=peer, device_id_type=MESH)
    pl.semaphore_wait(barrier, len(peers))


def gather_body(x, w, proj, logit, wo, xg, wf, sib, blk, rim, xs, xr, ws, wr, ss, sr, ps, pr, ls):
    s, z, core, cx, cy = place()
    a = jnp.where(core == 0, cx, cy)
    b = jnp.where(core == 0, cy, cx)

    def chip_of(da, db):
        ra, rb = (a + da) % 4, (b + db) % 4
        return jnp.where(core == 0, ra * YN + rb, rb * YN + ra)

    def dev_of(da, db):
        return (chip_of(da, db) * 2 + core, z)

    other = (s + 1 - 2 * core, z)
    right, left = (s, (z + 1) % TEN), (s, (z + TEN - 1) % TEN)
    after, before = ((s + 1) % SEQ, z), ((s + SEQ - 1) % SEQ, z)
    greet([other, right, left, dev_of(1, 0), dev_of(3, 0), dev_of(0, 1), dev_of(0, 3), after, before])

    pair = remote(w, sib, ps.at[0], pr.at[0], other)
    pair.start()
    own = pltpu.make_async_copy(x, xg.at[z], ls.at[0])
    own.start()

    def x_copy(d, k):
        c = (z + (TEN - k + 1 if d == 0 else k - 1)) % TEN
        if k == 4:
            here = xg.at[c, pl.ds(64 * d, 64)]
        else:
            here = xg.at[c]
        return remote(x if k == 1 else here, here, xs.at[d, k - 1], xr.at[d, k - 1], right if d == 0 else left)

    def x_recv(d, k):
        c = (z + (TEN - k if d == 0 else k)) % TEN
        here = xg.at[c, pl.ds(64 * d, 64)] if k == 4 else xg.at[c]
        return remote(here, here, xs.at[d, k - 1], xr.at[d, k - 1], right if d == 0 else left)

    for d in range(2):
        x_copy(d, 1).start()

    pair.wait_recv()
    mine = w[...].astype(f32)
    theirs = sib[...].astype(f32)
    blk[0:PIECE] = jnp.where(core == 0, mine, theirs)
    blk[PIECE:PAIR] = jnp.where(core == 0, theirs, mine)
    here = pl.multiple_of(chip_of(0, 0) * PAIR, 16)
    wf[pl.ds(here, PAIR)] = blk[...].astype(bf16)

    col0 = pl.multiple_of(core * HALF, 128)

    def w_ref(da, db, cols=None):
        return wf.at[pl.ds(pl.multiple_of(chip_of(da, db) * PAIR, 16), PAIR), pl.ds(col0 if cols is None else cols, HALF)]

    sends = []

    def w_send(da, db, ta, tb):
        ra, rb = (da - ta) % 4, (db - tb) % 4
        at = len(sends)
        copy = remote(w_ref(da, db), w_ref(da, db), ws.at[at], wr.at[ra * 4 + rb], dev_of(ta, tb))
        copy.start()
        sends.append(copy)

    def w_wait(da, db):
        remote(w_ref(da, db), w_ref(da, db), ws.at[0], wr.at[da * 4 + db], other).wait_recv()

    def across(da, db):
        copy = remote(w_ref(da, db), w_ref(da, db), ss.at[da * 4 + db], sr.at[da * 4 + db], other)
        copy.start()
        sends.append(copy)

    def hop_b(da):
        w_send(da, 0, 0, 1)
        w_send(da, 0, 0, 3)

    def x_forward(k):
        for d in range(2):
            x_recv(d, k).wait_recv()
            x_copy(d, k + 1).start()

    n_w = [0]
    w_send(0, 0, 1, 0)
    w_send(0, 0, 3, 0)
    hop_b(0)
    w_wait(3, 0)
    w_send(3, 0, 1, 0)
    hop_b(3)
    across(3, 0)
    w_wait(1, 0)
    hop_b(1)
    across(1, 0)
    w_wait(2, 0)
    hop_b(2)
    across(2, 0)
    w_wait(0, 3)
    w_send(0, 3, 0, 1)
    across(0, 3)
    w_wait(0, 1)
    across(0, 1)
    x_forward(1)
    for da, db in ((3, 1), (1, 3)):
        w_wait(da, db)
        w_send(da, db, 0, 3 if db == 1 else 1)
        across(da, db)
    for da, db in ((3, 3), (1, 1), (2, 1)):
        w_wait(da, db)
        if (da, db) == (2, 1):
            w_send(da, db, 0, 3)
        across(da, db)
    for da, db in ((2, 3), (0, 2), (3, 2), (1, 2), (2, 2)):
        w_wait(da, db)
        across(da, db)
    x_forward(2)
    colx = pl.multiple_of((1 - core) * HALF, 128)
    for i in range(1, 16):
        oa, ob = i // 4, i % 4
        ra, rb = ob, oa
        ref = w_ref(ra, rb, colx)
        remote(ref, ref, ss.at[i], sr.at[i], other).wait_recv()
    own.wait()
    keep = pltpu.make_async_copy(wf.at[:, pl.ds(OUT_AT, COLS - OUT_AT)], wo, ls.at[1])
    keep.start()

    rim_copy = remote(proj.at[pl.ds(TEN * CH, 16)], rim, ps.at[1], pr.at[1], after)

    def project(c):
        r = pl.multiple_of(16 + c * CH, 16)

        def tile(n, carry):
            at = pl.multiple_of(n * 256, 256)
            acc = jnp.dot(xg[c], wf[:, pl.ds(at, 256)], preferred_element_type=f32)
            proj[pl.ds(r, CH), pl.ds(at, 256)] = acc.astype(bf16)
            return carry

        lax.fori_loop(0, BETA_AT // 256, tile, 0)
        logit[pl.ds(pl.multiple_of(c * CH, CH), CH)] = jnp.dot(xg[c], wf[:, BETA_AT:BETA_AT + 128], preferred_element_type=f32)

        @pl.when((c == TEN - 1) & (s < SEQ - 1))
        def _():
            rim_copy.start()

    def around(k):
        def one(i, carry):
            project((z + jnp.where(i == 0, TEN - k, k)) % TEN)
            return carry
        lax.fori_loop(0, 2, one, 0)

    project(z)
    around(1)
    around(2)
    x_forward(3)
    around(3)
    for d in range(2):
        x_recv(d, 4).wait_recv()
    project((z + 4) % TEN)

    @pl.when(s > 0)
    def _():
        rim_copy.wait_recv()
        proj[0:16] = rim[...]

    @pl.when(s == 0)
    def _():
        proj[0:16] = jnp.zeros((16, BETA_AT), bf16)

    @pl.when(s < SEQ - 1)
    def _():
        rim_copy.wait_send()

    keep.wait()
    pair.wait_send()
    for copy in sends:
        copy.wait_send()
    for d in range(2):
        for k in range(1, 5):
            x_copy(d, k).wait_send()


def gather_project(x, w):
    return pl.pallas_call(
        gather_body,
        in_specs=[pl.BlockSpec(memory_space=pltpu.VMEM)] * 2,
        out_specs=[pl.BlockSpec(memory_space=pltpu.VMEM), pl.BlockSpec(memory_space=pltpu.VMEM), pl.BlockSpec(memory_space=pl.ANY)],
        out_shape=[
            jax.ShapeDtypeStruct((TEN * CH + 16, BETA_AT), bf16),
            jax.ShapeDtypeStruct((TEN * CH, 128), f32),
            jax.ShapeDtypeStruct((COLS, COLS - OUT_AT), bf16),
        ],
        scratch_shapes=[
            pltpu.VMEM((TEN, CH, COLS), bf16),
            pltpu.VMEM((COLS, COLS), bf16),
            pltpu.VMEM((PIECE, COLS), bf16),
            pltpu.VMEM((PAIR, COLS), f32),
            pltpu.VMEM((16, BETA_AT), bf16),
            pltpu.SemaphoreType.DMA((2, 4)),
            pltpu.SemaphoreType.DMA((2, 4)),
            pltpu.SemaphoreType.DMA((32,)),
            pltpu.SemaphoreType.DMA((16,)),
            pltpu.SemaphoreType.DMA((16,)),
            pltpu.SemaphoreType.DMA((16,)),
            pltpu.SemaphoreType.DMA((2,)),
            pltpu.SemaphoreType.DMA((2,)),
            pltpu.SemaphoreType.DMA((2,)),
        ],
        compiler_params=pltpu.CompilerParams(collective_id=0, has_side_effects=True, vmem_limit_bytes=56 << 20),
    )(x, w)


def finish_body(rd, lo, pb, gain, wo, out, sibpb, gy, pre, gx, ss, sb, sin, nrm, part, rsend, rrecv,
                csem, ysem, xsem, tsem, rssem, rrsem):
    s, z, core, cx, cy = place()
    other = (s + 1 - 2 * core, z)
    right, left = (s, (z + 1) % TEN), (s, (z + TEN - 1) % TEN)

    def y_dev(k):
        return ((cx * YN + (cy + k) % YN) * 2 + core, z)

    def x_dev(k):
        return ((((cx + k) % XN) * YN + cy) * 2 + core, z)

    greet([other, right, left] + [y_dev(k) for k in (1, 2, 3)] + [x_dev(k) for k in (1, 2, 3)])
    mine0, their0 = 2 * core, 2 - 2 * core
    first = remote(pb.at[pl.ds(their0, 2)], sibpb, csem.at[0], csem.at[1], other)
    first.start()

    def chain(later, earlier):
        p = mm(later[:, :HD], earlier)
        return p + jnp.concatenate([jnp.zeros((HD, HD), f32), later[:, HD:].astype(f32)], axis=1)

    first.wait_recv()
    heads = range(2)
    lead = []
    for i in heads:
        own, got = pb[mine0 + i], sibpb[i]
        head, tail = jnp.where(core == 0, own, got), jnp.where(core == 0, got, own)
        lead.append(head)
        gy[cy, i] = chain(tail, head).astype(bf16)
    y_copies = [remote(gy.at[cy], gy.at[cy], ysem.at[0, k], ysem.at[1, k], y_dev(k)) for k in (1, 2, 3)]
    for copy in y_copies:
        copy.start()
    for k in (1, 2, 3):
        slot = gy.at[(cy + YN - k) % YN]
        remote(slot, slot, ysem.at[0, k], ysem.at[1, k], y_dev(k)).wait_recv()
    eye = (lax.broadcasted_iota(jnp.int32, (HD, 2 * HD), 0) == lax.broadcasted_iota(jnp.int32, (HD, 2 * HD), 1)).astype(bf16)
    run = [gy[0, i] for i in heads]
    for i in heads:
        pre[0, i] = eye
        pre[1, i] = run[i]
    for k in (1, 2, 3):
        run = [chain(gy[k, i], run[i]).astype(bf16) for i in heads]
        for i in heads:
            if k < 3:
                pre[k + 1, i] = run[i]
            else:
                gx[cx, i] = run[i]
    x_copies = [remote(gx.at[cx], gx.at[cx], xsem.at[0, k], xsem.at[1, k], x_dev(k)) for k in (1, 2, 3)]
    for copy in x_copies:
        copy.start()
    for k in (1, 2, 3):
        slot = gx.at[(cx + XN - k) % XN]
        remote(slot, slot, xsem.at[0, k], xsem.at[1, k], x_dev(k)).wait_recv()
    state = [jnp.zeros((HD, HD), f32) for i in heads]
    for i in heads:
        ss[0, i] = state[i]
    for k in range(3):
        state = [mm(gx[k, i, :, :HD], state[i]) + gx[k, i, :, HD:].astype(f32) for i in heads]
        for i in heads:
            ss[k + 1, i] = state[i]
    for i in heads:
        entry = mm(pre[cy, i, :, :HD], ss[cx, i]) + pre[cy, i, :, HD:].astype(f32)
        behind = mm(lead[i][:, :HD], entry) + lead[i][:, HD:].astype(f32)
        sin[mine0 + i] = jnp.where(core == 0, entry, behind).astype(bf16)
        sb[i] = jnp.where(core == 0, behind, entry).astype(bf16)
    last = remote(sb, sin.at[pl.ds(mine0, 2)], csem.at[2], csem.at[3], other)
    last.start()
    their = sin.at[pl.ds(their0, 2)]
    remote(their, their, csem.at[2], csem.at[3], other).wait_recv()

    def attend(c):
        r = pl.ds(pl.multiple_of(c * CH, CH), CH)
        att = [mm(rd[r, h * HD:(h + 1) * HD], sin[h]) + lo[r, h * HD:(h + 1) * HD].astype(f32) for h in range(4)]
        for h in range(4):
            scale = lax.rsqrt(jnp.mean(att[h] * att[h], axis=-1, keepdims=True) + 1e-5)
            nrm[c, :, h * HD:(h + 1) * HD] = (att[h] * scale * gain[...]).astype(bf16)

    def partial(d, c):
        for n in range(0, HALF, 384):
            part[d, :, n:n + 384] = mm_nt(nrm[c], wo[d * HALF + n:d * HALF + n + 384])

    def chunk(d, t):
        return (z + (2 * TEN - 1 - t if d == 0 else 1 + t)) % TEN

    def send(d, t, u):
        rows = pl.ds(u * 64, 64)
        return remote(rsend.at[d, t, rows], rrecv.at[d, t, rows], rssem.at[d, t, u], rrsem.at[d, t, u], right if d == 0 else left)

    for d in range(2):
        c = chunk(d, 0)
        attend(c)
        partial(d, c)
        for u in range(2):
            rsend[d, 0, u * 64:u * 64 + 64] = part[d, u * 64:u * 64 + 64].astype(bf16)
            send(d, 0, u).start()

    def step(t, carry):
        for d in range(2):
            c = chunk(d, t)

            @pl.when((t < 3) | ((t == 3) & (d == 0)))
            def _():
                attend(c)

            partial(d, c)
        for u in range(2):
            for d in range(2):
                send(d, t - 1, u).wait_recv()
                total = part[d, u * 64:u * 64 + 64] + rrecv[d, t - 1, u * 64:u * 64 + 64].astype(f32)
                rsend[d, t, u * 64:u * 64 + 64] = total.astype(bf16)
                send(d, t, u).start()
        return carry

    lax.fori_loop(1, 7, step, 0)
    attend(z)
    for d in range(2):
        partial(d, z)
    for u in range(2):
        for d in range(2):
            send(d, 6, u).wait_recv()
            total = part[d, u * 64:u * 64 + 64] + rrecv[d, 6, u * 64:u * 64 + 64].astype(f32)
            out[u * 64:u * 64 + 64, d * HALF:(d + 1) * HALF] = total.astype(bf16)

    first.wait_send()
    last.wait_send()
    for copy in y_copies + x_copies:
        copy.wait_send()

    def drain(t, carry):
        for d in range(2):
            for u in range(2):
                send(d, t, u).wait_send()
        return carry

    lax.fori_loop(0, 7, drain, 0)


def finish(rd, lo, pb, gain, wo):
    return pl.pallas_call(
        finish_body,
        in_specs=[pl.BlockSpec(memory_space=pltpu.VMEM)] * 5,
        out_specs=pl.BlockSpec(memory_space=pltpu.VMEM),
        out_shape=jax.ShapeDtypeStruct((CH, COLS), bf16),
        scratch_shapes=[
            pltpu.VMEM((2, HD, 2 * HD), bf16),
            pltpu.VMEM((YN, 2, HD, 2 * HD), bf16),
            pltpu.VMEM((YN, 2, HD, 2 * HD), bf16),
            pltpu.VMEM((XN, 2, HD, 2 * HD), bf16),
            pltpu.VMEM((XN, 2, HD, HD), f32),
            pltpu.VMEM((2, HD, HD), bf16),
            pltpu.VMEM((4, HD, HD), bf16),
            pltpu.VMEM((TEN, CH, 4 * HD), bf16),
            pltpu.VMEM((2, CH, HALF), f32),
            pltpu.VMEM((2, 7, CH, HALF), bf16),
            pltpu.VMEM((2, 7, CH, HALF), bf16),
            pltpu.SemaphoreType.DMA((4,)),
            pltpu.SemaphoreType.DMA((2, 4)),
            pltpu.SemaphoreType.DMA((2, 4)),
            pltpu.SemaphoreType.DMA((2,)),
            pltpu.SemaphoreType.DMA((2, 7, 2)),
            pltpu.SemaphoreType.DMA((2, 7, 2)),
        ],
        compiler_params=pltpu.CompilerParams(collective_id=1, has_side_effects=True, vmem_limit_bytes=56 << 20),
    )(rd, lo, pb, gain, wo)


def per_device(x_rows, w_qkv, w_beta, conv_weight, log_decay, norm_gain, w_out):
    packed = jnp.concatenate(
        [w_qkv.reshape(PIECE, BETA_AT), jnp.pad(w_beta, ((0, 0), (0, OUT_AT - BETA_AT - w_beta.shape[1]))), w_out.T], axis=1)
    proj, logit, wo = gather_project(x_rows, packed)
    rd, lo, pb = k2(proj, logit, log_decay, conv_weight.reshape(4, BETA_AT))
    return finish(rd, lo, pb, norm_gain.reshape(1, HD), wo)


def solution(mesh):
    in_specs = (
        P(("seq", "tensor"), None),
        P("seq", None, "tensor"),
        P("seq", "tensor"),
        P(None, None, "tensor"),
        P("seq", "tensor"),
        P(),
        P("tensor", "seq"),
    )
    return jax.shard_map(per_device, mesh=mesh, in_specs=in_specs, out_specs=P(("seq", "tensor"), None), check_vma=False)
```

```python
import functools
import jax
import jax.numpy as jnp
from jax import lax
from jax.experimental import pallas as pl
from jax.experimental.pallas import tpu as pltpu
from jax.sharding import PartitionSpec as P

f32, bf16 = jnp.float32, jnp.bfloat16
CH = 128
HD = 128


def mm(a, b):
    return jnp.dot(a.astype(bf16), b.astype(bf16), preferred_element_type=f32)


def mm_nt(a, b):
    return lax.dot_general(a.astype(bf16), b.astype(bf16), (((1,), (1,)), ((), ())), preferred_element_type=f32)


def mm_tn(a, b):
    return lax.dot_general(a.astype(bf16), b.astype(bf16), (((0,), (0,)), ((), ())), preferred_element_type=f32)


def chunk_terms(heads, chunks, load_proj, load_gate, strength, taps):
    row = lax.broadcasted_iota(jnp.int32, (CH, CH), 0)
    col = lax.broadcasted_iota(jnp.int32, (CH, CH), 1)
    incl, strict = row >= col, row > col
    lower = incl.astype(bf16)
    each = range(heads * chunks)
    width = heads * HD

    def conv(part, h):
        at = part * width + (h % heads) * HD
        p = load_proj(h // heads, at).astype(f32)
        y = taps[3:4, at:at + HD] * p[16:]
        for j in range(3):
            y = y + taps[j:j + 1, at:at + HD] * p[13 + j:13 + j + CH]
        return y * (0.5 + 0.5 * jnp.tanh(0.5 * y))

    def unit(m):
        return m * lax.rsqrt(jnp.sum(m * m, axis=-1, keepdims=True) + 1e-6)

    q = [unit(conv(0, h)) for h in each]
    k = [unit(conv(1, h)) for h in each]
    v = [conv(2, h) for h in each]
    b = [strength[h // heads][:, h % heads:h % heads + 1] for h in each]
    g = [load_gate(h // heads, h % heads) for h in each]
    ghi = [m.astype(bf16) for m in g]
    glo = [(g[h] - ghi[h].astype(f32)).astype(bf16) for h in each]
    cum = [mm(lower, ghi[h]) + mm(lower, glo[h]) for h in each]
    mid = [m[CH // 2 - 1:CH // 2] for m in cum]
    fin = [m[CH - 1:CH] for m in cum]
    up = [jnp.exp(cum[h] - mid[h]) for h in each]
    down = [jnp.exp(mid[h] - cum[h]) for h in each]
    emid = [jnp.exp(mid[h]) for h in each]
    k_up = [k[h] * up[h] for h in each]
    q_up = [q[h] * up[h] for h in each]
    k_down = [k[h] * down[h] for h in each]
    k_end = [k_down[h] * jnp.exp(fin[h] - mid[h]) for h in each]
    both = [mm_nt(jnp.concatenate([k_up[h], q_up[h]], axis=0), k_down[h]) for h in each]
    mix = [jnp.where(strict, b[h] * both[h][:CH], 0.0).astype(bf16) for h in each]
    score = [jnp.where(incl, both[h][CH:], 0.0).astype(bf16) for h in each]
    zero = jnp.zeros((CH, CH), bf16)

    def off(n):
        return ((row // (2 * n)) == (col // (2 * n))) & ((row // n) % 2 == 1) & ((col // n) % 2 == 0)

    near = (row // 16) == (col // 16)
    flat = []
    for h in each:
        m = jnp.where(near, mix[h].astype(f32), 0.0)
        total = m[0:16]
        for r in range(16, CH, 16):
            total = total + m[r:r + 16]
        flat.append(total.astype(bf16))
    flat = jnp.concatenate(flat, axis=0)
    row16 = lax.broadcasted_iota(jnp.int32, (16, CH), 0)
    col16 = lax.broadcasted_iota(jnp.int32, (16, CH), 1)
    small = [(row16 == col16 % 16).astype(f32) for h in each]
    for j in range(15):
        spread = mm(flat, near & ((row % 16) == j))
        small = [small[h] - spread[16 * h:16 * h + 16] * small[h][j:j + 1] for h in each]
    inv = [jnp.where(near, jnp.concatenate([small[h]] * (CH // 16), axis=0), 0.0) for h in each]
    n = 16
    while n < CH:
        m = off(n)
        part = [jnp.where(m, mix[h], zero) for h in each]
        low = [inv[h].astype(bf16) for h in each]
        step = [mm(part[h], low[h]).astype(bf16) for h in each]
        inv = [inv[h] - mm(low[h], step[h]) for h in each]
        n *= 2
    q_dec = [q_up[h] * emid[h] for h in each]
    rhs = [jnp.concatenate([b[h] * (k_up[h] * emid[h]), b[h] * v[h]], axis=1).astype(bf16) for h in each]
    wu = [mm(inv[h], rhs[h]).astype(bf16) for h in each]
    sw = [mm(score[h], wu[h]) for h in each]
    kw = [mm_tn(k_end[h], wu[h]) for h in each]
    reader = [q_dec[h] - sw[h][:, :HD] for h in each]
    local = [sw[h][:, HD:] for h in each]
    erase = [kw[h][:, :HD] for h in each]
    inject = [kw[h][:, HD:] for h in each]
    final = [jnp.sum(jnp.where(row == col, jnp.exp(fin[h]), 0.0), axis=1, keepdims=True) for h in each]
    return reader, local, erase, inject, final


MESH = pl.DeviceIdType.MESH
XN, YN = 4, 4
SEQ, TEN = 32, 8
PIECE = 72
PAIR = 2 * PIECE
COLS = 2304
HALF = COLS // 2
HEADS = 4
WIDTH = HEADS * HD
BETA_AT = 1536
OUT_AT = 1792


def place():
    s, z = lax.axis_index("seq"), lax.axis_index("tensor")
    core, chip = s % 2, s // 2
    return s, z, core, chip // YN, chip % YN


def remote(src, dst, ssem, rsem, to):
    copy = pltpu.make_async_remote_copy(src_ref=src, dst_ref=dst, send_sem=ssem, recv_sem=rsem, device_id=to, device_id_type=MESH)
    return copy


def greet(peers):
    barrier = pltpu.get_barrier_semaphore()
    for peer in peers:
        pl.semaphore_signal(barrier, inc=1, device_id=peer, device_id_type=MESH)
    pl.semaphore_wait(barrier, len(peers))


def layer_body(x, w, gate_in, taps, gain, out,
               xg, wf, wo, sib, blk, rim, proj, logit, gate, rdr, loc, ers, inj, fin, pbs, run, pb, rd, lo,
               sibpb, gy, pre, gx, ss_, sb, sin, nrm, part, rsend, rrecv,
               xs, xr, ws, wr, ss, sr, ps, pr, ls, csem, ysem, xsem, rssem, rrsem):
    s, z, core, cx, cy = place()
    a = jnp.where(core == 0, cx, cy)
    b = jnp.where(core == 0, cy, cx)

    def chip_of(da, db):
        ra, rb = (a + da) % 4, (b + db) % 4
        return jnp.where(core == 0, ra * YN + rb, rb * YN + ra)

    def dev_of(da, db):
        return (chip_of(da, db) * 2 + core, z)

    other = (s + 1 - 2 * core, z)
    right, left = (s, (z + 1) % TEN), (s, (z + TEN - 1) % TEN)
    after, before = ((s + 1) % SEQ, z), ((s + SEQ - 1) % SEQ, z)
    def y_dev(k):
        return ((cx * YN + (cy + k) % YN) * 2 + core, z)

    def x_dev(k):
        return ((((cx + k) % XN) * YN + cy) * 2 + core, z)

    greet([other, right, left, after, before] + [y_dev(k) for k in (1, 2, 3)] + [x_dev(k) for k in (1, 2, 3)])

    pair = remote(w, sib, ps.at[0], pr.at[0], other)
    pair.start()
    own = pltpu.make_async_copy(x, xg.at[z], ls.at[0])
    own.start()
    decay = pltpu.make_async_copy(gate_in, gate, ls.at[1])
    decay.start()

    def x_copy(d, k):
        c = (z + (TEN - k + 1 if d == 0 else k - 1)) % TEN
        if k == 4:
            here = xg.at[c, pl.ds(64 * d, 64)]
        else:
            here = xg.at[c]
        return remote(x if k == 1 else here, here, xs.at[d, k - 1], xr.at[d, k - 1], right if d == 0 else left)

    def x_recv(d, k):
        c = (z + (TEN - k if d == 0 else k)) % TEN
        here = xg.at[c, pl.ds(64 * d, 64)] if k == 4 else xg.at[c]
        return remote(here, here, xs.at[d, k - 1], xr.at[d, k - 1], right if d == 0 else left)

    for d in range(2):
        x_copy(d, 1).start()

    pair.wait_recv()
    mine = w[...].astype(f32)
    theirs = sib[...].astype(f32)
    blk[0:PIECE] = jnp.where(core == 0, mine, theirs)
    blk[PIECE:PAIR] = jnp.where(core == 0, theirs, mine)
    here = pl.multiple_of(chip_of(0, 0) * PAIR, 16)
    wf[pl.ds(here, PAIR)] = blk[:, :OUT_AT].astype(bf16)
    wo[pl.ds(here, PAIR)] = blk[:, OUT_AT:].astype(bf16)

    def w_ref(g, da, db, who=core):
        full, n = (wf, OUT_AT // 2) if g == 0 else (wo, (COLS - OUT_AT) // 2)
        rows = pl.ds(pl.multiple_of(chip_of(da, db) * PAIR, 16), PAIR)
        return full.at[rows, pl.ds(pl.multiple_of(who * n, 128), n)]

    sends = []
    used = [0, 0]

    def w_send(g, da, db, ta, tb):
        ra, rb = (da - ta) % 4, (db - tb) % 4
        n = used[g]
        used[g] += 1

        def copy():
            ref = w_ref(g, da, db)
            return remote(ref, ref, ws.at[g, n], wr.at[g, ra * 4 + rb], dev_of(ta, tb))

        copy().start()
        sends.append(copy)

    def w_wait(g, da, db):
        ref = w_ref(g, da, db)
        remote(ref, ref, ws.at[g, 0], wr.at[g, da * 4 + db], other).wait_recv()

    def across(g, da, db):
        def copy():
            ref = w_ref(g, da, db)
            return remote(ref, ref, ss.at[g, da * 4 + db], sr.at[g, da * 4 + db], other)

        copy().start()
        sends.append(copy)

    def hop_b(g, da):
        w_send(g, da, 0, 0, 1)
        w_send(g, da, 0, 0, 3)

    def first_hops(g):
        w_send(g, 0, 0, 1, 0)
        w_send(g, 0, 0, 3, 0)
        hop_b(g, 0)

    def relay_hops(g, blocks):
        for da, db in blocks:
            w_wait(g, da, db)
            if (da, db) == (3, 0):
                w_send(g, da, db, 1, 0)
            if db == 0:
                hop_b(g, da)
            if (db == 3 and da < 2) or (db == 1 and da > 1):
                w_send(g, da, db, 0, 1 if db == 3 else 3)
            across(g, da, db)

    def other_half(g):
        for i in range(1, 16):
            ref = w_ref(g, i % 4, i // 4, 1 - core)
            remote(ref, ref, ss.at[g, i], sr.at[g, i], other).wait_recv()

    def x_forward(k):
        for d in range(2):
            x_recv(d, k).wait_recv()
            x_copy(d, k + 1).start()

    near_blocks = [(3, 0), (1, 0), (2, 0), (0, 3), (0, 1)]
    side_blocks = [(3, 1), (1, 3), (3, 3), (1, 1)]
    far_blocks = [(2, 1), (2, 3), (0, 2), (3, 2), (1, 2), (2, 2)]
    first_hops(0)
    relay_hops(0, near_blocks)
    x_forward(1)
    relay_hops(0, side_blocks)
    relay_hops(0, far_blocks)
    first_hops(1)
    x_forward(2)
    other_half(0)
    own.wait()
    decay.wait()

    rim_copy = remote(proj.at[pl.ds(TEN * CH, 16)], rim, ps.at[1], pr.at[1], after)

    @pl.when(s == 0)
    def _():
        proj[0:16] = jnp.zeros((16, BETA_AT), bf16)

    def project(c):
        r = pl.multiple_of(16 + c * CH, 16)

        def tile(n, carry):
            at = pl.multiple_of(n * 768, 256)
            acc = jnp.dot(xg[c], wf[:, pl.ds(at, 768)], preferred_element_type=f32)
            proj[pl.ds(r, CH), pl.ds(at, 768)] = acc.astype(bf16)
            return carry

        lax.fori_loop(0, BETA_AT // 768, tile, 0)
        logit[pl.ds(pl.multiple_of(c * CH, CH), CH)] = jnp.dot(xg[c], wf[:, BETA_AT:BETA_AT + 128], preferred_element_type=f32)

        @pl.when((c == TEN - 1) & (s < SEQ - 1))
        def _():
            rim_copy.start()

    def terms(k):
        chunks = [(z + TEN - k) % TEN, (z + k + 1) % TEN]
        at = [pl.multiple_of(c * CH, CH) for c in chunks]

        @pl.when((s > 0) & ((chunks[0] == 0) | (chunks[1] == 0)))
        def _():
            rim_copy.wait_recv()
            proj[0:16] = rim[...]

        reader, local, erase, inject, final = chunk_terms(
            HEADS, 2,
            lambda i, col: proj[pl.ds(at[i], CH + 16), col:col + HD],
            lambda i, h: gate[pl.ds(at[i], CH), h * HD:(h + 1) * HD],
            [1.0 / (1.0 + jnp.exp(-logit[pl.ds(at[i], CH)])) for i in range(2)],
            taps)
        for i in range(2):
            for h in range(HEADS):
                n = i * HEADS + h
                rdr[chunks[i], h] = reader[n].astype(bf16)
                loc[chunks[i], h] = local[n]
                ers[chunks[i], h] = erase[n].astype(bf16)
                inj[chunks[i], h] = inject[n]
                fin[chunks[i], h] = final[n]

    project(z)

    def step(k, carry):
        @pl.when(k == 2)
        def _():
            x_forward(3)

        @pl.when(k < 3)
        def _():
            def one(i, carry):
                project((z + jnp.where(i == 0, TEN - 1 - k, k + 1)) % TEN)
                return carry
            lax.fori_loop(0, 2, one, 0)

        @pl.when(k == 3)
        def _():
            for d in range(2):
                x_recv(d, 4).wait_recv()
            project((z + 4) % TEN)

        for n, blocks in enumerate((near_blocks, side_blocks, far_blocks)):
            @pl.when(k == n)
            def _():
                relay_hops(1, blocks)

        terms(k)
        return carry

    lax.fori_loop(0, 4, step, 0)
    other_half(1)

    eye2 = (lax.broadcasted_iota(jnp.int32, (HD, 2 * HD), 0) == lax.broadcasted_iota(jnp.int32, (HD, 2 * HD), 1)).astype(bf16)
    zeros = jnp.zeros((HD, HD), f32)
    for h in range(HEADS):
        run[h] = eye2.astype(f32)

    def fold(c, carry):
        for h in range(HEADS):
            now = run[h]
            short = now.astype(bf16)
            pbs[c, h] = short
            run[h] = fin[c, h] * now - mm(ers[c, h], short) + jnp.concatenate([zeros, inj[c, h]], axis=1)
        return carry

    lax.fori_loop(0, TEN, fold, 0)
    for h in range(HEADS):
        pb[h] = run[h].astype(bf16)

    def unfold(c, carry):
        r = pl.ds(pl.multiple_of(c * CH, CH), CH)
        for h in range(HEADS):
            both = mm(rdr[c, h], pbs[c, h])
            rd[r, h * HD:(h + 1) * HD] = both[:, :HD].astype(bf16)
            lo[r, h * HD:(h + 1) * HD] = both[:, HD:] + loc[c, h]
        return carry

    mine0, their0 = 2 * core, 2 - 2 * core
    first = remote(pb.at[pl.ds(their0, 2)], sibpb, csem.at[0], csem.at[1], other)
    first.start()

    def chain(later, earlier):
        p = mm(later[:, :HD], earlier)
        return p + jnp.concatenate([jnp.zeros((HD, HD), f32), later[:, HD:].astype(f32)], axis=1)

    first.wait_recv()
    heads = range(2)
    lead = []
    for i in heads:
        own, got = pb[mine0 + i], sibpb[i]
        head, tail = jnp.where(core == 0, own, got), jnp.where(core == 0, got, own)
        lead.append(head)
        gy[cy, i] = chain(tail, head).astype(bf16)
    y_copies = [remote(gy.at[cy], gy.at[cy], ysem.at[0, k], ysem.at[1, k], y_dev(k)) for k in (1, 2, 3)]
    for copy in y_copies:
        copy.start()
    lax.fori_loop(0, TEN, unfold, 0)
    for k in (1, 2, 3):
        slot = gy.at[(cy + YN - k) % YN]
        remote(slot, slot, ysem.at[0, k], ysem.at[1, k], y_dev(k)).wait_recv()
    acc = [gy[0, i] for i in heads]
    for i in heads:
        pre[0, i] = eye2
        pre[1, i] = acc[i]
    for k in (1, 2, 3):
        acc = [chain(gy[k, i], acc[i]).astype(bf16) for i in heads]
        for i in heads:
            if k < 3:
                pre[k + 1, i] = acc[i]
            else:
                gx[cx, i] = acc[i]
    x_copies = [remote(gx.at[cx], gx.at[cx], xsem.at[0, k], xsem.at[1, k], x_dev(k)) for k in (1, 2, 3)]
    for copy in x_copies:
        copy.start()
    for k in (1, 2, 3):
        slot = gx.at[(cx + XN - k) % XN]
        remote(slot, slot, xsem.at[0, k], xsem.at[1, k], x_dev(k)).wait_recv()
    state = [jnp.zeros((HD, HD), f32) for i in heads]
    for i in heads:
        ss_[0, i] = state[i]
    for k in range(3):
        state = [mm(gx[k, i, :, :HD], state[i]) + gx[k, i, :, HD:].astype(f32) for i in heads]
        for i in heads:
            ss_[k + 1, i] = state[i]
    for i in heads:
        entry = mm(pre[cy, i, :, :HD], ss_[cx, i]) + pre[cy, i, :, HD:].astype(f32)
        behind = mm(lead[i][:, :HD], entry) + lead[i][:, HD:].astype(f32)
        sin[mine0 + i] = jnp.where(core == 0, entry, behind).astype(bf16)
        sb[i] = jnp.where(core == 0, behind, entry).astype(bf16)
    last = remote(sb, sin.at[pl.ds(mine0, 2)], csem.at[2], csem.at[3], other)
    last.start()
    their = sin.at[pl.ds(their0, 2)]
    remote(their, their, csem.at[2], csem.at[3], other).wait_recv()

    def attend(c):
        r = pl.ds(pl.multiple_of(c * CH, CH), CH)
        att = [mm(rd[r, h * HD:(h + 1) * HD], sin[h]) + lo[r, h * HD:(h + 1) * HD] for h in range(4)]
        for h in range(4):
            scale = lax.rsqrt(jnp.mean(att[h] * att[h], axis=-1, keepdims=True) + 1e-5)
            nrm[c, :, h * HD:(h + 1) * HD] = (att[h] * scale * gain[...]).astype(bf16)

    def partial(d, c):
        for n in range(0, HALF, 384):
            part[d, :, n:n + 384] = mm_nt(nrm[c], wo[d * HALF + n:d * HALF + n + 384])

    def chunk(d, t):
        return (z + (2 * TEN - 1 - t if d == 0 else 1 + t)) % TEN

    def send(d, t, u):
        rows = pl.ds(u * 64, 64)
        return remote(rsend.at[d, t, rows], rrecv.at[d, t, rows], rssem.at[d, t, u], rrsem.at[d, t, u], right if d == 0 else left)

    for d in range(2):
        c = chunk(d, 0)
        attend(c)
        partial(d, c)
        for u in range(2):
            rsend[d, 0, u * 64:u * 64 + 64] = part[d, u * 64:u * 64 + 64].astype(bf16)
            send(d, 0, u).start()

    def ring(t, carry):
        for d in range(2):
            c = chunk(d, t)

            @pl.when((t < 3) | ((t == 3) & (d == 0)))
            def _():
                attend(c)

            partial(d, c)
        for u in range(2):
            for d in range(2):
                send(d, t - 1, u).wait_recv()
                total = part[d, u * 64:u * 64 + 64] + rrecv[d, t - 1, u * 64:u * 64 + 64].astype(f32)
                rsend[d, t, u * 64:u * 64 + 64] = total.astype(bf16)
                send(d, t, u).start()
        return carry

    lax.fori_loop(1, 7, ring, 0)
    attend(z)
    for d in range(2):
        partial(d, z)
    for u in range(2):
        for d in range(2):
            send(d, 6, u).wait_recv()
            total = part[d, u * 64:u * 64 + 64] + rrecv[d, 6, u * 64:u * 64 + 64].astype(f32)
            out[u * 64:u * 64 + 64, d * HALF:(d + 1) * HALF] = total.astype(bf16)

    @pl.when(s < SEQ - 1)
    def _():
        rim_copy.wait_send()

    pair.wait_send()
    for copy in sends:
        copy().wait_send()
    for d in range(2):
        for k in range(1, 5):
            x_copy(d, k).wait_send()
    first.wait_send()
    last.wait_send()
    for copy in y_copies + x_copies:
        copy.wait_send()

    def drain(t, carry):
        for d in range(2):
            for u in range(2):
                send(d, t, u).wait_send()
        return carry

    lax.fori_loop(0, 7, drain, 0)


def layer(x, w, gate, taps, gain):
    vm, dma = pltpu.VMEM, pltpu.SemaphoreType.DMA
    whole = pl.BlockSpec(memory_space=pltpu.VMEM)
    return pl.pallas_call(
        layer_body,
        in_specs=[whole, whole, pl.BlockSpec(memory_space=pl.ANY), whole, whole],
        out_specs=whole,
        out_shape=jax.ShapeDtypeStruct((CH, COLS), bf16),
        scratch_shapes=[
            vm((TEN, CH, COLS), bf16),
            vm((COLS, OUT_AT), bf16),
            vm((COLS, WIDTH), bf16),
            vm((PIECE, COLS), bf16),
            vm((PAIR, COLS), f32),
            vm((16, BETA_AT), bf16),
            vm((TEN * CH + 16, BETA_AT), bf16),
            vm((TEN * CH, 128), f32),
            vm((TEN * CH, WIDTH), f32),
            vm((TEN, HEADS, CH, HD), bf16),
            vm((TEN, HEADS, CH, HD), f32),
            vm((TEN, HEADS, HD, HD), bf16),
            vm((TEN, HEADS, HD, HD), f32),
            vm((TEN, HEADS, HD, 1), f32),
            vm((TEN, HEADS, HD, 2 * HD), bf16),
            vm((HEADS, HD, 2 * HD), f32),
            vm((HEADS, HD, 2 * HD), bf16),
            vm((TEN * CH, WIDTH), bf16),
            vm((TEN * CH, WIDTH), f32),
            vm((2, HD, 2 * HD), bf16),
            vm((YN, 2, HD, 2 * HD), bf16),
            vm((YN, 2, HD, 2 * HD), bf16),
            vm((XN, 2, HD, 2 * HD), bf16),
            vm((XN, 2, HD, HD), f32),
            vm((2, HD, HD), bf16),
            vm((4, HD, HD), bf16),
            vm((TEN, CH, WIDTH), bf16),
            vm((2, CH, HALF), f32),
            vm((2, 7, CH, HALF), bf16),
            vm((2, 7, CH, HALF), bf16),
            dma((2, 4)), dma((2, 4)), dma((2, 16)), dma((2, 16)), dma((2, 16)), dma((2, 16)),
            dma((2,)), dma((2,)), dma((2,)), dma((4,)), dma((2, 4)), dma((2, 4)), dma((2, 7, 2)), dma((2, 7, 2)),
        ],
        compiler_params=pltpu.CompilerParams(collective_id=0, has_side_effects=True, vmem_limit_bytes=62 << 20),
    )(x, w, gate, taps, gain)


def per_device(x_rows, w_qkv, w_beta, conv_weight, log_decay, norm_gain, w_out):
    packed = jnp.concatenate(
        [w_qkv.reshape(PIECE, BETA_AT), jnp.pad(w_beta, ((0, 0), (0, OUT_AT - BETA_AT - w_beta.shape[1]))), w_out.T], axis=1)
    return layer(x_rows, packed, log_decay, conv_weight.reshape(4, BETA_AT), norm_gain.reshape(1, HD))


def solution(mesh):
    in_specs = (
        P(("seq", "tensor"), None),
        P("seq", None, "tensor"),
        P("seq", "tensor"),
        P(None, None, "tensor"),
        P("seq", "tensor"),
        P(),
        P("tensor", "seq"),
    )
    return jax.shard_map(per_device, mesh=mesh, in_specs=in_specs, out_specs=P(("seq", "tensor"), None), check_vma=False)
```

```python
import functools
import jax
import jax.numpy as jnp
from jax import lax
from jax.experimental import pallas as pl
from jax.experimental.pallas import tpu as pltpu
from jax.sharding import PartitionSpec as P

f32, bf16 = jnp.float32, jnp.bfloat16
CH = 128
HD = 128


def mm(a, b):
    return jnp.dot(a.astype(bf16), b.astype(bf16), preferred_element_type=f32)


def mm_nt(a, b):
    return lax.dot_general(a.astype(bf16), b.astype(bf16), (((1,), (1,)), ((), ())), preferred_element_type=f32)


def mm_tn(a, b):
    return lax.dot_general(a.astype(bf16), b.astype(bf16), (((0,), (0,)), ((), ())), preferred_element_type=f32)


def triangle():
    row = lax.broadcasted_iota(jnp.int32, (CH, CH), 0)
    col = lax.broadcasted_iota(jnp.int32, (CH, CH), 1)
    return row, col


def short_conv(p, taps, at):
    p = p.astype(f32)
    y = taps[3:4, at:at + HD] * p[16:]
    for j in range(3):
        y = y + taps[j:j + 1, at:at + HD] * p[13 + j:13 + j + CH]
    return y * (0.5 + 0.5 * jnp.tanh(0.5 * y))


def unit(m):
    return m * lax.rsqrt(jnp.sum(m * m, axis=-1, keepdims=True) + 1e-6)


def unit_lower_inverse(mix):
    row, col = triangle()
    each = range(len(mix))
    near = (row // 16) == (col // 16)
    flat = []
    for h in each:
        m = jnp.where(near, mix[h].astype(f32), 0.0)
        total = m[0:16]
        for r in range(16, CH, 16):
            total = total + m[r:r + 16]
        flat.append(total.astype(bf16))
    flat = jnp.concatenate(flat, axis=0)
    row16 = lax.broadcasted_iota(jnp.int32, (16, CH), 0)
    col16 = lax.broadcasted_iota(jnp.int32, (16, CH), 1)
    small = [(row16 == col16 % 16).astype(f32) for h in each]
    for j in range(15):
        spread = mm(flat, near & ((row % 16) == j))
        small = [small[h] - spread[16 * h:16 * h + 16] * small[h][j:j + 1] for h in each]
    inv = [jnp.where(near, jnp.concatenate([small[h]] * (CH // 16), axis=0), 0.0) for h in each]
    zero = jnp.zeros((CH, CH), bf16)
    n = 16
    while n < CH:
        off = ((row // (2 * n)) == (col // (2 * n))) & ((row // n) % 2 == 1) & ((col // n) % 2 == 0)
        part = [jnp.where(off, mix[h], zero) for h in each]
        low = [inv[h].astype(bf16) for h in each]
        step = [mm(part[h], low[h]).astype(bf16) for h in each]
        inv = [inv[h] - mm(low[h], step[h]) for h in each]
        n *= 2
    return [inv[h].astype(bf16) for h in each]


def key_terms(keys, strength, decay):
    row, col = triangle()
    lower = (row >= col).astype(bf16)
    each = range(len(keys))
    k = [unit(m) for m in keys]
    ghi = [m.astype(bf16) for m in decay]
    glo = [(decay[h] - ghi[h].astype(f32)).astype(bf16) for h in each]
    cum = [mm(lower, ghi[h]) + mm(lower, glo[h]) for h in each]
    mid = [m[CH // 2 - 1:CH // 2] for m in cum]
    fin = [m[CH - 1:CH] for m in cum]
    rel = [cum[h] - mid[h] for h in each]
    k_up = [k[h] * jnp.exp(rel[h]) for h in each]
    k_down = [k[h] * jnp.exp(-rel[h]) for h in each]
    k_end = [(k_down[h] * jnp.exp(fin[h] - mid[h])).astype(bf16) for h in each]
    k_down = [m.astype(bf16) for m in k_down]
    mix = [mm_nt(k_up[h], k_down[h]) for h in each]
    mix = [jnp.where(row > col, strength[h] * mix[h], 0.0).astype(bf16) for h in each]
    inv = unit_lower_inverse(mix)
    emid = [jnp.exp(m) for m in mid]
    w = [mm(inv[h], strength[h] * (k_up[h] * emid[h])).astype(bf16) for h in each]
    erase = [mm_tn(k_end[h], w[h]).astype(bf16) for h in each]
    final = [jnp.sum(jnp.where(row == col, jnp.exp(fin[h]), 0.0), axis=1, keepdims=True) for h in each]
    return rel, emid, k_down, k_end, inv, w, erase, final


def value_terms(values, strength, k_end, inv):
    each = range(len(values))
    u = [mm(inv[h], strength[h] * values[h]).astype(bf16) for h in each]
    inject = [mm_tn(k_end[h], u[h]) for h in each]
    return u, inject


def read_terms(query, rel, emid, k_down, w, u):
    row, col = triangle()
    each = range(len(query))
    q = [unit(query[h]) * jnp.exp(rel[h]) for h in each]
    score = [jnp.where(row >= col, mm_nt(q[h], k_down[h]), 0.0).astype(bf16) for h in each]
    sw = [mm(score[h], jnp.concatenate([w[h], u[h]], axis=1)) for h in each]
    reader = [(q[h] * emid[h] - sw[h][:, :HD]).astype(bf16) for h in each]
    local = [sw[h][:, HD:] for h in each]
    return reader, local


MESH = pl.DeviceIdType.MESH
XN, YN = 4, 4
SEQ, TEN = 32, 8
PIECE = 72
PAIR = 2 * PIECE
COLS = 2304
HALF = COLS // 2
HEADS = 4
WIDTH = HEADS * HD
QKV = 1536
BETA_AT = 512
V_AT = 768
Q_AT = 1280
OUT_AT = 1792


def place():
    s, z = lax.axis_index("seq"), lax.axis_index("tensor")
    core, chip = s % 2, s // 2
    return s, z, core, chip // YN, chip % YN


def remote(src, dst, ssem, rsem, to):
    copy = pltpu.make_async_remote_copy(src_ref=src, dst_ref=dst, send_sem=ssem, recv_sem=rsem, device_id=to, device_id_type=MESH)
    return copy


def greet(peers):
    barrier = pltpu.get_barrier_semaphore()
    for peer in peers:
        pl.semaphore_signal(barrier, inc=1, device_id=peer, device_id_type=MESH)
    pl.semaphore_wait(barrier, len(peers))


def layer_body(x, w_qkv, w_beta, w_out, gate_in, taps, gain, out,
               xg, wf, w, sib, blk, rim, proj, logit, gate, emid, kdn, ken, inv, wk, uv, rdr, loc, ers, inj, fin, pbs, run, pb, rd, lo,
               gc, pre, gx, begin, sb, sin, nrm, part, rsend, rrecv,
               xs, xr, ws, wr, ss, sr, ps, pr, ls, upsem, xsem, downsem, rssem, rrsem):
    s, z, core, cx, cy = place()
    a = jnp.where(core == 0, cx, cy)
    b = jnp.where(core == 0, cy, cx)

    def chip_of(da, db):
        ra, rb = (a + da) % 4, (b + db) % 4
        return jnp.where(core == 0, ra * YN + rb, rb * YN + ra)

    def dev_of(da, db):
        return (chip_of(da, db) * 2 + core, z)

    other = (s + 1 - 2 * core, z)
    right, left = (s, (z + 1) % TEN), (s, (z + TEN - 1) % TEN)
    after, before = ((s + 1) % SEQ, z), ((s + SEQ - 1) % SEQ, z)
    def column_dev(i):
        return ((cx * YN + i // 2) * 2 + i % 2, z)

    def x_dev(k):
        return ((((cx + k) % XN) * YN + cy) * 2 + core, z)

    me = cy * 2 + core
    greet([right, left, after, before] + [x_dev(k) for k in (1, 2, 3)] + [column_dev((me + k) % 8) for k in range(1, 8)])

    def x_copy(d, k, i):
        c, r = (z + (TEN - k + 1 if d == 0 else k - 1)) % TEN, pl.ds(64 * i, 64)
        here = xg.at[c, r]
        return remote(x.at[r] if k == 1 else here, here, xs.at[d, k - 1, i], xr.at[d, k - 1, i], right if d == 0 else left)

    def x_recv(d, k, i):
        here = xg.at[(z + (TEN - k if d == 0 else k)) % TEN, pl.ds(64 * i, 64)]
        return remote(here, here, xs.at[d, k - 1, i], xr.at[d, k - 1, i], right if d == 0 else left)

    for i in range(2):
        for d in range(2):
            x_copy(d, 1, i ^ d).start()

    w[:, :BETA_AT] = w_qkv[1]
    spread = (lax.broadcasted_iota(jnp.int32, (HEADS, V_AT - BETA_AT), 0) == lax.broadcasted_iota(jnp.int32, (HEADS, V_AT - BETA_AT), 1))
    w[:, BETA_AT:V_AT] = mm_tn(w_beta[...], spread).astype(bf16)
    w[:, V_AT:Q_AT] = w_qkv[2]
    w[:, Q_AT:OUT_AT] = w_qkv[0]
    w[:, OUT_AT:] = w_out[...]
    pair = remote(w, sib, ps.at[0], pr.at[0], other)
    pair.start()
    own = pltpu.make_async_copy(x, xg.at[z], ls.at[0])
    own.start()
    decay = pltpu.make_async_copy(gate_in, gate, ls.at[1])
    decay.start()
    pair.wait_recv()
    mine = w[...].astype(f32)
    theirs = sib[...].astype(f32)
    blk[0:PIECE] = jnp.where(core == 0, mine, theirs)
    blk[PIECE:PAIR] = jnp.where(core == 0, theirs, mine)
    here = pl.multiple_of(chip_of(0, 0) * PAIR, 16)
    wf[pl.ds(here, PAIR)] = blk[...].astype(bf16)

    def w_ref(g, da, db, who=core):
        full, first, n = ((wf, 0, Q_AT // 2), (wf, Q_AT, (COLS - Q_AT) // 2))[g]
        rows = pl.ds(pl.multiple_of(chip_of(da, db) * PAIR, 16), PAIR)
        return full.at[rows, pl.ds(pl.multiple_of(first + who * n, 128), n)]

    sends = []
    used = [0] * 2

    def w_send(g, da, db, ta, tb):
        ra, rb = (da - ta) % 4, (db - tb) % 4
        n = used[g]
        used[g] += 1

        def copy():
            ref = w_ref(g, da, db)
            return remote(ref, ref, ws.at[g, n], wr.at[g, ra * 4 + rb], dev_of(ta, tb))

        copy().start()
        sends.append(copy)

    def w_wait(g, da, db):
        ref = w_ref(g, da, db)
        remote(ref, ref, ws.at[g, 0], wr.at[g, da * 4 + db], other).wait_recv()

    def across(g, da, db):
        def copy():
            ref = w_ref(g, da, db)
            return remote(ref, ref, ss.at[g, da * 4 + db], sr.at[g, da * 4 + db], other)

        copy().start()
        sends.append(copy)

    def hop_b(g, da):
        w_send(g, da, 0, 0, 1)
        w_send(g, da, 0, 0, 3)

    def first_hops(g):
        w_send(g, 0, 0, 1, 0)
        w_send(g, 0, 0, 3, 0)
        hop_b(g, 0)

    def relay_hops(g, blocks):
        for da, db in blocks:
            w_wait(g, da, db)
            if (da, db) == (3, 0):
                w_send(g, da, db, 1, 0)
            if db == 0:
                hop_b(g, da)
            if (db == 3 and da < 2) or (db == 1 and da > 1):
                w_send(g, da, db, 0, 1 if db == 3 else 3)
            across(g, da, db)

    def other_half(g):
        for i in range(1, 16):
            ref = w_ref(g, i % 4, i // 4, 1 - core)
            remote(ref, ref, ss.at[g, i], sr.at[g, i], other).wait_recv()

    def x_forward(k, i):
        for d in range(2):
            x_recv(d, k, i ^ d).wait_recv()
            if k < 3 or i == 0:
                x_copy(d, k + 1, i ^ d).start()

    rims = []
    for n in range(3):
        cols = pl.ds(n * WIDTH, WIDTH)
        rims.append(remote(proj.at[pl.ds(TEN * CH, 16), cols], rim.at[:, cols], ps.at[1 + n], pr.at[1 + n], after))

    @pl.when(s == 0)
    def _():
        proj[0:16] = jnp.zeros((16, QKV), bf16)

    def project(c, part):
        r = pl.multiple_of(16 + c * CH, 16)
        at = (0, V_AT, Q_AT)[part]
        acc = jnp.dot(xg[c], wf[:, at:at + WIDTH], preferred_element_type=f32)
        proj[pl.ds(r, CH), part * WIDTH:(part + 1) * WIDTH] = acc.astype(bf16)
        if part == 0:
            acc = jnp.dot(xg[c], wf[:, BETA_AT:BETA_AT + 128], preferred_element_type=f32)
            logit[pl.ds(pl.multiple_of(c * CH, CH), CH)] = acc

        @pl.when((c == TEN - 1) & (s < SEQ - 1))
        def _():
            rims[part].start()

    def pair_of(k):
        chunks = [(z + TEN - k) % TEN, (z + k + 1) % TEN]
        return chunks, [pl.multiple_of(c * CH, CH) for c in chunks], [(i, h) for i in range(2) for h in range(HEADS)]

    def rim_in(chunks, part):
        @pl.when((s > 0) & ((chunks[0] == 0) | (chunks[1] == 0)))
        def _():
            rims[part].wait_recv()
            proj[0:16, part * WIDTH:(part + 1) * WIDTH] = rim[:, part * WIDTH:(part + 1) * WIDTH]

    def strengths(at):
        b = [1.0 / (1.0 + jnp.exp(-logit[pl.ds(at[i], CH)])) for i in range(2)]
        return [b[i][:, h:h + 1] for i in range(2) for h in range(HEADS)]

    def conv(at, i, h, part):
        col, tap = part * WIDTH + h * HD, ((1, 2, 0)[part]) * WIDTH + h * HD
        return short_conv(proj[pl.ds(at[i], CH + 16), col:col + HD], taps, tap)

    def put(chunks, each, refs, got):
        for n, (i, h) in enumerate(each):
            for ref, value in zip(refs, got):
                ref[chunks[i], h] = value[n]

    def take(chunks, each, *refs):
        return [[ref[chunks[i], h] for i, h in each] for ref in refs]

    def decays(at, each):
        return [gate[pl.ds(at[i], CH), h * HD:(h + 1) * HD] for i, h in each]

    def keys_of(k):
        chunks, at, each = pair_of(k)
        rim_in(chunks, 0)
        got = key_terms([conv(at, i, h, 0) for i, h in each], strengths(at), decays(at, each))
        for n, (i, h) in enumerate(each):
            gate[pl.ds(at[i], CH), h * HD:(h + 1) * HD] = got[0][n]
        put(chunks, each, (emid, kdn, ken, inv, wk, ers, fin), got[1:])

    def values_of(k):
        chunks, at, each = pair_of(k)
        rim_in(chunks, 1)
        got = value_terms([conv(at, i, h, 1) for i, h in each], strengths(at), *take(chunks, each, ken, inv))
        put(chunks, each, (uv, inj), got)

    def reads_of(k):
        chunks, at, each = pair_of(k)
        rim_in(chunks, 2)
        got = read_terms([conv(at, i, h, 2) for i, h in each], decays(at, each), *take(chunks, each, emid, kdn, wk, uv))
        put(chunks, each, (rdr, loc), got)

    near_blocks = [(3, 0), (1, 0), (0, 3), (0, 1)]
    side_blocks = [(2, 0), (3, 1), (1, 3), (3, 3), (1, 1)]
    far_blocks = [(2, 1), (2, 3), (0, 2), (3, 2), (1, 2), (2, 2)]
    first_hops(0)
    x_forward(1, 0)
    relay_hops(0, near_blocks)
    first_hops(1)
    x_forward(1, 1)
    relay_hops(0, side_blocks)
    relay_hops(1, near_blocks)
    x_forward(2, 0)
    relay_hops(0, far_blocks)
    x_forward(2, 1)
    own.wait()
    decay.wait()
    other_half(0)

    def nth(n):
        return (z + TEN + jnp.where(n % 2 == 1, -((n + 1) // 2), n // 2)) % TEN

    def many(part, lo_n, hi_n):
        def one(n, carry):
            project(nth(n), part)
            return carry
        lax.fori_loop(lo_n, hi_n, one, 0)

    def pairs(f, lo_n, hi_n):
        def one(n, carry):
            f(n)
            return carry
        lax.fori_loop(lo_n, hi_n, one, 0)

    def step(t, carry):
        when = lambda n: pl.when(t == n)

        @when(2)
        def _():
            x_forward(3, 1)

        @when(3)
        def _():
            for d in range(2):
                x_recv(d, 4, d).wait_recv()

        lo_n = jnp.where(t == 0, 0, 2 * t + 1)
        hi_n = jnp.minimum(2 * t + 3, TEN)
        many(0, lo_n, hi_n)
        many(1, lo_n, hi_n)

        @when(0)
        def _():
            relay_hops(1, side_blocks)

        keys_of(t)
        values_of(t)

        @when(0)
        def _():
            x_forward(3, 0)

        @when(1)
        def _():
            relay_hops(1, far_blocks)

        return carry

    lax.fori_loop(0, 4, step, 0)

    eye2 = (lax.broadcasted_iota(jnp.int32, (HD, 2 * HD), 0) == lax.broadcasted_iota(jnp.int32, (HD, 2 * HD), 1)).astype(bf16)
    zeros = jnp.zeros((HD, HD), f32)
    for h in range(HEADS):
        run[h] = eye2.astype(f32)

    def fold(c, carry):
        for h in range(HEADS):
            now = run[h]
            short = now.astype(bf16)
            pbs[c, h] = short
            run[h] = fin[c, h] * now - mm(ers[c, h], short) + jnp.concatenate([zeros, inj[c, h]], axis=1)
        return carry

    lax.fori_loop(0, TEN, fold, 0)
    for h in range(HEADS):
        pb[h] = run[h].astype(bf16)

    def unfold(c, carry):
        r = pl.ds(pl.multiple_of(c * CH, CH), CH)
        for h in range(HEADS):
            both = mm(rdr[c, h], pbs[c, h])
            rd[r, h * HD:(h + 1) * HD] = both[:, :HD].astype(bf16)
            lo[r, h * HD:(h + 1) * HD] = both[:, HD:] + loc[c, h]
        return carry

    def chain(later, earlier):
        p = mm(later[:, :HD], earlier)
        return (p + jnp.concatenate([zeros, later[:, HD:].astype(f32)], axis=1)).astype(bf16)

    chains = core == 0

    def up(h):
        return remote(pb.at[h], gc.at[me], upsem.at[0, h], upsem.at[1, me], column_dev(2 * h))

    def along(k):
        return remote(gx.at[cx], gx.at[cx], xsem.at[0, k], xsem.at[1, k], x_dev(k))

    def down(i):
        return remote(sb.at[i], sin.at[cy], downsem.at[0, i], downsem.at[1, cy], column_dev(i))

    def keeps(h):
        return chains & (cy == h)

    for h in range(HEADS):
        @pl.when(keeps(h))
        def _():
            gc[me] = pb[h]

        @pl.when(jnp.logical_not(keeps(h)))
        def _():
            up(h).start()

    other_half(1)
    many(2, 0, TEN)
    pairs(reads_of, 0, 4)

    @pl.when(chains)
    def _():
        for i in range(8):
            @pl.when(me != i)
            def _():
                remote(gc.at[i], gc.at[i], upsem.at[0, 0], upsem.at[1, i], column_dev(0)).wait_recv()
        two = [chain(gc[i + 1], gc[i]) for i in range(0, 8, 2)]
        four = [chain(two[1], two[0]), chain(two[3], two[2])]
        gx[cx] = chain(four[1], four[0])
        for k in (1, 2, 3):
            along(k).start()
        pre[0] = eye2
        pre[1] = gc[0]
        pre[2] = two[0]
        pre[3] = chain(gc[2], two[0])
        pre[4] = four[0]
        pre[5] = chain(gc[4], four[0])
        six = chain(two[2], four[0])
        pre[6] = six
        pre[7] = chain(gc[6], six)

    lax.fori_loop(0, TEN, unfold, 0)

    @pl.when(chains)
    def _():
        for k in (1, 2, 3):
            slot = gx.at[(cx + XN - k) % XN]
            remote(slot, slot, xsem.at[0, k], xsem.at[1, k], x_dev(k)).wait_recv()
        state = zeros
        begin[0] = state
        for k in range(XN - 1):
            state = mm(gx[k, :, :HD], state) + gx[k, :, HD:].astype(f32)
            begin[k + 1] = state
        state = begin[cx]
        for i in range(8):
            sb[i] = (mm(pre[i, :, :HD], state) + pre[i, :, HD:].astype(f32)).astype(bf16)

            @pl.when(me == i)
            def _():
                sin[cy] = sb[i]

            @pl.when(me != i)
            def _():
                down(i).start()

    for h in range(HEADS):
        @pl.when(jnp.logical_not(keeps(h)))
        def _():
            remote(sin.at[h], sin.at[h], downsem.at[0, 0], downsem.at[1, h], column_dev(0)).wait_recv()

    def attend(c):
        r = pl.ds(pl.multiple_of(c * CH, CH), CH)
        att = [mm(rd[r, h * HD:(h + 1) * HD], sin[h]) + lo[r, h * HD:(h + 1) * HD] for h in range(4)]
        for h in range(4):
            scale = lax.rsqrt(jnp.mean(att[h] * att[h], axis=-1, keepdims=True) + 1e-5)
            nrm[c, :, h * HD:(h + 1) * HD] = (att[h] * scale * gain[...]).astype(bf16)

    def partial(d, c):
        def tile(n, carry):
            at = pl.multiple_of(n * 384, 128)
            part[d, :, pl.ds(at, 384)] = mm_nt(nrm[c], wf[pl.ds(pl.multiple_of(d * HALF + at, 128), 384), OUT_AT:])
            return carry
        lax.fori_loop(0, HALF // 384, tile, 0)

    def send(d, t, u):
        rows = pl.ds(u * 64, 64)
        return remote(rsend.at[d, t, rows], rrecv.at[d, t, rows], rssem.at[d, t, u], rrsem.at[d, t, u], right if d == 0 else left)

    def ring(t, carry):
        def work(d, carry):
            c = (z + jnp.where(d == 0, 2 * TEN - 1 - t, 1 + t)) % TEN

            @pl.when((t < 3) | ((t == 3) & (d == 0)) | ((t == 7) & (d == 0)))
            def _():
                attend(c)

            partial(d, c)
            return carry

        lax.fori_loop(0, 2, work, 0)
        for u in range(2):
            rows = pl.ds(u * 64, 64)
            for d in range(2):
                @pl.when(t > 0)
                def _():
                    send(d, t - 1, u).wait_recv()
                    part[d, rows] += rrecv[d, t - 1, rows].astype(f32)

                @pl.when(t < 7)
                def _():
                    rsend[d, t, rows] = part[d, rows].astype(bf16)
                    send(d, t, u).start()
        return carry

    lax.fori_loop(0, 8, ring, 0)
    for d in range(2):
        out[:, d * HALF:(d + 1) * HALF] = part[d].astype(bf16)

    @pl.when(s < SEQ - 1)
    def _():
        for copy in rims:
            copy.wait_send()

    pair.wait_send()
    for copy in sends:
        copy().wait_send()
    for d in range(2):
        for k in range(1, 5):
            for i in range(2):
                if k < 4 or i == d:
                    x_copy(d, k, i).wait_send()
    for h in range(HEADS):
        @pl.when(jnp.logical_not(keeps(h)))
        def _():
            up(h).wait_send()

    @pl.when(chains)
    def _():
        for k in (1, 2, 3):
            along(k).wait_send()
        for i in range(8):
            @pl.when(me != i)
            def _():
                down(i).wait_send()


    def drain(t, carry):
        for d in range(2):
            for u in range(2):
                send(d, t, u).wait_send()
        return carry

    lax.fori_loop(0, 7, drain, 0)


def layer(x, w_qkv, w_beta, w_out, gate, taps, gain):
    vm, dma = pltpu.VMEM, pltpu.SemaphoreType.DMA
    whole = pl.BlockSpec(memory_space=pltpu.VMEM)
    return pl.pallas_call(
        layer_body,
        in_specs=[whole] * 4 + [pl.BlockSpec(memory_space=pl.ANY), whole, whole],
        out_specs=whole,
        out_shape=jax.ShapeDtypeStruct((CH, COLS), bf16),
        scratch_shapes=[
            vm((TEN, CH, COLS), bf16),
            vm((COLS, COLS), bf16),
            vm((PIECE, COLS), bf16),
            vm((PIECE, COLS), bf16),
            vm((PAIR, COLS), f32),
            vm((16, QKV), bf16),
            vm((TEN * CH + 16, QKV), bf16),
            vm((TEN * CH, 128), f32),
            vm((TEN * CH, WIDTH), f32),
            vm((TEN, HEADS, 1, HD), f32),
            vm((TEN, HEADS, CH, HD), bf16),
            vm((TEN, HEADS, CH, HD), bf16),
            vm((TEN, HEADS, CH, HD), bf16),
            vm((TEN, HEADS, CH, HD), bf16),
            vm((TEN, HEADS, CH, HD), bf16),
            vm((TEN, HEADS, CH, HD), bf16),
            vm((TEN, HEADS, CH, HD), f32),
            vm((TEN, HEADS, HD, HD), bf16),
            vm((TEN, HEADS, HD, HD), f32),
            vm((TEN, HEADS, HD, 1), f32),
            vm((TEN, HEADS, HD, 2 * HD), bf16),
            vm((HEADS, HD, 2 * HD), f32),
            vm((HEADS, HD, 2 * HD), bf16),
            vm((TEN * CH, WIDTH), bf16),
            vm((TEN * CH, WIDTH), f32),
            vm((8, HD, 2 * HD), bf16),
            vm((8, HD, 2 * HD), bf16),
            vm((XN, HD, 2 * HD), bf16),
            vm((XN, HD, HD), f32),
            vm((8, HD, HD), bf16),
            vm((HEADS, HD, HD), bf16),
            vm((TEN, CH, WIDTH), bf16),
            vm((2, CH, HALF), f32),
            vm((2, 7, CH, HALF), bf16),
            vm((2, 7, CH, HALF), bf16),
            dma((2, 4, 2)), dma((2, 4, 2)), dma((2, 16)), dma((2, 16)), dma((2, 16)), dma((2, 16)),
            dma((4,)), dma((4,)), dma((2,)), dma((2, 8)), dma((2, 4)), dma((2, 8)), dma((2, 7, 2)), dma((2, 7, 2)),
        ],
        compiler_params=pltpu.CompilerParams(collective_id=0, has_side_effects=True, vmem_limit_bytes=62 << 20),
    )(x, w_qkv, w_beta, w_out, gate, taps, gain)


def per_device(x_rows, w_qkv, w_beta, conv_weight, log_decay, norm_gain, w_out):
    return layer(x_rows, w_qkv.transpose(1, 0, 2), w_beta.T, w_out.T, log_decay, conv_weight.reshape(4, QKV), norm_gain.reshape(1, HD))


def solution(mesh):
    in_specs = (
        P(("seq", "tensor"), None),
        P("seq", None, "tensor"),
        P("seq", "tensor"),
        P(None, None, "tensor"),
        P("seq", "tensor"),
        P(),
        P("tensor", "seq"),
    )
    return jax.shard_map(per_device, mesh=mesh, in_specs=in_specs, out_specs=P(("seq", "tensor"), None), check_vma=False)
```

```python
import functools
import jax
import jax.numpy as jnp
from jax import lax
from jax.experimental import pallas as pl
from jax.experimental.pallas import tpu as pltpu
from jax.sharding import PartitionSpec as P

f32, bf16 = jnp.float32, jnp.bfloat16
CH = 128
HD = 128


def mm(a, b):
    return jnp.dot(a.astype(bf16), b.astype(bf16), preferred_element_type=f32)


def mm_nt(a, b):
    return lax.dot_general(a.astype(bf16), b.astype(bf16), (((1,), (1,)), ((), ())), preferred_element_type=f32)


def mm_tn(a, b):
    return lax.dot_general(a.astype(bf16), b.astype(bf16), (((0,), (0,)), ((), ())), preferred_element_type=f32)


def triangle():
    row = lax.broadcasted_iota(jnp.int32, (CH, CH), 0)
    col = lax.broadcasted_iota(jnp.int32, (CH, CH), 1)
    return row, col


def short_conv(p, taps, at):
    p = p.astype(f32)
    y = taps[3:4, at:at + HD] * p[16:]
    for j in range(3):
        y = y + taps[j:j + 1, at:at + HD] * p[13 + j:13 + j + CH]
    return y * (0.5 + 0.5 * jnp.tanh(0.5 * y))


def unit(m):
    return m * lax.rsqrt(jnp.sum(m * m, axis=-1, keepdims=True) + 1e-6)


def unit_lower_inverse(mix):
    row, col = triangle()
    each = range(len(mix))
    near = (row // 16) == (col // 16)
    flat = []
    for h in each:
        m = jnp.where(near, mix[h].astype(f32), 0.0)
        total = m[0:16]
        for r in range(16, CH, 16):
            total = total + m[r:r + 16]
        flat.append(total.astype(bf16))
    flat = jnp.concatenate(flat, axis=0)
    row16 = lax.broadcasted_iota(jnp.int32, (16, CH), 0)
    col16 = lax.broadcasted_iota(jnp.int32, (16, CH), 1)
    small = [(row16 == col16 % 16).astype(f32) for h in each]
    for j in range(15):
        spread = mm(flat, near & ((row % 16) == j))
        small = [small[h] - spread[16 * h:16 * h + 16] * small[h][j:j + 1] for h in each]
    inv = [jnp.where(near, jnp.concatenate([small[h]] * (CH // 16), axis=0), 0.0) for h in each]
    zero = jnp.zeros((CH, CH), bf16)
    n = 16
    while n < CH:
        off = ((row // (2 * n)) == (col // (2 * n))) & ((row // n) % 2 == 1) & ((col // n) % 2 == 0)
        part = [jnp.where(off, mix[h], zero) for h in each]
        low = [inv[h].astype(bf16) for h in each]
        step = [mm(part[h], low[h]).astype(bf16) for h in each]
        inv = [inv[h] - mm(low[h], step[h]) for h in each]
        n *= 2
    return [inv[h].astype(bf16) for h in each]


def key_terms(keys, strength, decay):
    row, col = triangle()
    lower = (row >= col).astype(bf16)
    each = range(len(keys))
    k = [unit(m) for m in keys]
    ghi = [m.astype(bf16) for m in decay]
    glo = [(decay[h] - ghi[h].astype(f32)).astype(bf16) for h in each]
    cum = [mm(lower, ghi[h]) + mm(lower, glo[h]) for h in each]
    mid = [m[CH // 2 - 1:CH // 2] for m in cum]
    fin = [m[CH - 1:CH] for m in cum]
    rel = [cum[h] - mid[h] for h in each]
    k_up = [k[h] * jnp.exp(rel[h]) for h in each]
    k_down = [k[h] * jnp.exp(-rel[h]) for h in each]
    k_end = [(k_down[h] * jnp.exp(fin[h] - mid[h])).astype(bf16) for h in each]
    k_down = [m.astype(bf16) for m in k_down]
    mix = [mm_nt(k_up[h], k_down[h]) for h in each]
    mix = [jnp.where(row > col, strength[h] * mix[h], 0.0).astype(bf16) for h in each]
    inv = unit_lower_inverse(mix)
    emid = [jnp.exp(m) for m in mid]
    w = [mm(inv[h], strength[h] * (k_up[h] * emid[h])).astype(bf16) for h in each]
    erase = [mm_tn(k_end[h], w[h]).astype(bf16) for h in each]
    final = [jnp.sum(jnp.where(row == col, jnp.exp(fin[h]), 0.0), axis=1, keepdims=True) for h in each]
    return rel, emid, k_down, k_end, inv, w, erase, final


def value_terms(values, strength, k_end, inv):
    each = range(len(values))
    u = [mm(inv[h], strength[h] * values[h]).astype(bf16) for h in each]
    inject = [mm_tn(k_end[h], u[h]) for h in each]
    return u, inject


def read_terms(query, rel, emid, k_down, w, u):
    row, col = triangle()
    each = range(len(query))
    q = [unit(query[h]) * jnp.exp(rel[h]) for h in each]
    score = [jnp.where(row >= col, mm_nt(q[h], k_down[h]), 0.0).astype(bf16) for h in each]
    sw = [mm(score[h], jnp.concatenate([w[h], u[h]], axis=1)) for h in each]
    reader = [(q[h] * emid[h] - sw[h][:, :HD]).astype(bf16) for h in each]
    local = [sw[h][:, HD:] for h in each]
    return reader, local


MESH = pl.DeviceIdType.MESH
XN, YN = 4, 4
SEQ, TEN = 32, 8
PIECE = 72
PAIR = 2 * PIECE
COLS = 2304
HALF = COLS // 2
HEADS = 4
WIDTH = HEADS * HD
QKV = 1536
BETA_AT = 512
V_AT = 768
Q_AT = 1280
OUT_AT = 1792


def place():
    s, z = lax.axis_index("seq"), lax.axis_index("tensor")
    core, chip = s % 2, s // 2
    return s, z, core, chip // YN, chip % YN


def remote(src, dst, ssem, rsem, to):
    copy = pltpu.make_async_remote_copy(src_ref=src, dst_ref=dst, send_sem=ssem, recv_sem=rsem, device_id=to, device_id_type=MESH)
    return copy


def greet(peers):
    barrier = pltpu.get_barrier_semaphore()
    for peer in peers:
        pl.semaphore_signal(barrier, inc=1, device_id=peer, device_id_type=MESH)
    pl.semaphore_wait(barrier, len(peers))


def layer_body(x, w_qkv, w_beta, w_out, gate_in, taps, gain, out,
               xg, wf, w, sib, blk, rim, proj, logit, gate, emid, kdn, ken, inv, wk, uv, rdr, loc, ers, inj, fin, pbs, run, pb, rd, lo,
               gc, pre, gx, begin, sb, sin, nrm, part, rsend, rrecv,
               xs, xr, ws, wr, ss, sr, ps, pr, ls, upsem, xsem, downsem, rssem, rrsem):
    s, z, core, cx, cy = place()
    a = jnp.where(core == 0, cx, cy)
    b = jnp.where(core == 0, cy, cx)

    def chip_of(da, db):
        ra, rb = (a + da) % 4, (b + db) % 4
        return jnp.where(core == 0, ra * YN + rb, rb * YN + ra)

    def dev_of(da, db):
        return (chip_of(da, db) * 2 + core, z)

    other = (s + 1 - 2 * core, z)
    right, left = (s, (z + 1) % TEN), (s, (z + TEN - 1) % TEN)
    after, before = ((s + 1) % SEQ, z), ((s + SEQ - 1) % SEQ, z)
    def column_dev(i):
        return ((cx * YN + i // 2) * 2 + i % 2, z)

    def x_dev(k):
        return ((((cx + k) % XN) * YN + cy) * 2 + core, z)

    me = cy * 2 + core
    greet([right, left, after, before] + [x_dev(k) for k in (1, 2, 3)] + [column_dev((me + k) % 8) for k in range(1, 8)])

    def x_copy(d, k, i):
        c, r = (z + (TEN - k + 1 if d == 0 else k - 1)) % TEN, pl.ds(64 * i, 64)
        here = xg.at[c, r]
        return remote(x.at[r] if k == 1 else here, here, xs.at[d, k - 1, i], xr.at[d, k - 1, i], right if d == 0 else left)

    def x_recv(d, k, i):
        here = xg.at[(z + (TEN - k if d == 0 else k)) % TEN, pl.ds(64 * i, 64)]
        return remote(here, here, xs.at[d, k - 1, i], xr.at[d, k - 1, i], right if d == 0 else left)

    w[:, :BETA_AT] = w_qkv[1]
    spread = (lax.broadcasted_iota(jnp.int32, (HEADS, V_AT - BETA_AT), 0) == lax.broadcasted_iota(jnp.int32, (HEADS, V_AT - BETA_AT), 1))
    w[:, BETA_AT:V_AT] = mm_tn(w_beta[...], spread).astype(bf16)
    w[:, V_AT:Q_AT] = w_qkv[2]
    w[:, Q_AT:OUT_AT] = w_qkv[0]
    w[:, OUT_AT:] = w_out[...]
    pair = remote(w, sib, ps.at[0], pr.at[0], other)
    pair.start()
    for i in range(2):
        for d in range(2):
            x_copy(d, 1, i ^ d).start()

    own = pltpu.make_async_copy(x, xg.at[z], ls.at[0])
    own.start()
    decay = pltpu.make_async_copy(gate_in, gate, ls.at[1])
    decay.start()
    pair.wait_recv()
    mine = w[...].astype(f32)
    theirs = sib[...].astype(f32)
    blk[0:PIECE] = jnp.where(core == 0, mine, theirs)
    blk[PIECE:PAIR] = jnp.where(core == 0, theirs, mine)
    here = pl.multiple_of(chip_of(0, 0) * PAIR, 16)
    wf[pl.ds(here, PAIR)] = blk[...].astype(bf16)

    def w_ref(g, da, db, who=core):
        full, first, n = ((wf, 0, Q_AT // 2), (wf, Q_AT, (COLS - Q_AT) // 2))[g]
        rows = pl.ds(pl.multiple_of(chip_of(da, db) * PAIR, 16), PAIR)
        return full.at[rows, pl.ds(pl.multiple_of(first + who * n, 128), n)]

    sends = []
    used = [0] * 2

    def w_send(g, da, db, ta, tb):
        ra, rb = (da - ta) % 4, (db - tb) % 4
        n = used[g]
        used[g] += 1

        def copy():
            ref = w_ref(g, da, db)
            return remote(ref, ref, ws.at[g, n], wr.at[g, ra * 4 + rb], dev_of(ta, tb))

        copy().start()
        sends.append(copy)

    def w_wait(g, da, db):
        ref = w_ref(g, da, db)
        remote(ref, ref, ws.at[g, 0], wr.at[g, da * 4 + db], other).wait_recv()

    def across(g, da, db):
        def copy():
            ref = w_ref(g, da, db)
            return remote(ref, ref, ss.at[g, da * 4 + db], sr.at[g, da * 4 + db], other)

        copy().start()
        sends.append(copy)

    def hop_b(g, da):
        w_send(g, da, 0, 0, 1)
        w_send(g, da, 0, 0, 3)

    def first_hops(g):
        w_send(g, 0, 0, 1, 0)
        w_send(g, 0, 0, 3, 0)
        hop_b(g, 0)

    def relay_hops(g, blocks):
        for da, db in blocks:
            w_wait(g, da, db)
            if (da, db) == (3, 0):
                w_send(g, da, db, 1, 0)
            if db == 0:
                hop_b(g, da)
            if (db == 3 and da < 2) or (db == 1 and da > 1):
                w_send(g, da, db, 0, 1 if db == 3 else 3)
            across(g, da, db)

    def other_half(g):
        for i in range(1, 16):
            ref = w_ref(g, i % 4, i // 4, 1 - core)
            remote(ref, ref, ss.at[g, i], sr.at[g, i], other).wait_recv()

    def x_forward(k, i):
        for d in range(2):
            x_recv(d, k, i ^ d).wait_recv()
            if k < 3 or i == 0:
                x_copy(d, k + 1, i ^ d).start()

    rims = []
    for n in range(3):
        cols = pl.ds(n * WIDTH, WIDTH)
        rims.append(remote(proj.at[pl.ds(TEN * CH, 16), cols], rim.at[:, cols], ps.at[1 + n], pr.at[1 + n], after))

    @pl.when(s == 0)
    def _():
        proj[0:16] = jnp.zeros((16, QKV), bf16)

    def project(c, part):
        r = pl.multiple_of(16 + c * CH, 16)
        at = (0, V_AT, Q_AT)[part]
        acc = jnp.dot(xg[c], wf[:, at:at + WIDTH], preferred_element_type=f32)
        proj[pl.ds(r, CH), part * WIDTH:(part + 1) * WIDTH] = acc.astype(bf16)
        if part == 0:
            acc = jnp.dot(xg[c], wf[:, BETA_AT:BETA_AT + 128], preferred_element_type=f32)
            logit[pl.ds(pl.multiple_of(c * CH, CH), CH)] = acc

        @pl.when((c == TEN - 1) & (s < SEQ - 1))
        def _():
            rims[part].start()

    def pair_of(k):
        chunks = [(z + TEN - k) % TEN, (z + k + 1) % TEN]
        return chunks, [pl.multiple_of(c * CH, CH) for c in chunks], [(i, h) for i in range(2) for h in range(HEADS)]

    def rim_in(chunks, part):
        @pl.when((s > 0) & ((chunks[0] == 0) | (chunks[1] == 0)))
        def _():
            rims[part].wait_recv()
            proj[0:16, part * WIDTH:(part + 1) * WIDTH] = rim[:, part * WIDTH:(part + 1) * WIDTH]

    def strengths(at):
        b = [1.0 / (1.0 + jnp.exp(-logit[pl.ds(at[i], CH)])) for i in range(2)]
        return [b[i][:, h:h + 1] for i in range(2) for h in range(HEADS)]

    def conv(at, i, h, part):
        col, tap = part * WIDTH + h * HD, ((1, 2, 0)[part]) * WIDTH + h * HD
        return short_conv(proj[pl.ds(at[i], CH + 16), col:col + HD], taps, tap)

    def put(chunks, each, refs, got):
        for n, (i, h) in enumerate(each):
            for ref, value in zip(refs, got):
                ref[chunks[i], h] = value[n]

    def take(chunks, each, *refs):
        return [[ref[chunks[i], h] for i, h in each] for ref in refs]

    def decays(at, each):
        return [gate[pl.ds(at[i], CH), h * HD:(h + 1) * HD] for i, h in each]

    def keys_of(k):
        chunks, at, each = pair_of(k)
        rim_in(chunks, 0)
        got = key_terms([conv(at, i, h, 0) for i, h in each], strengths(at), decays(at, each))
        for n, (i, h) in enumerate(each):
            gate[pl.ds(at[i], CH), h * HD:(h + 1) * HD] = got[0][n]
        put(chunks, each, (emid, kdn, ken, inv, wk, ers, fin), got[1:])

    def values_of(k):
        chunks, at, each = pair_of(k)
        rim_in(chunks, 1)
        got = value_terms([conv(at, i, h, 1) for i, h in each], strengths(at), *take(chunks, each, ken, inv))
        put(chunks, each, (uv, inj), got)

    def reads_of(k):
        chunks, at, each = pair_of(k)
        rim_in(chunks, 2)
        got = read_terms([conv(at, i, h, 2) for i, h in each], decays(at, each), *take(chunks, each, emid, kdn, wk, uv))
        put(chunks, each, (rdr, loc), got)

    near_blocks = [(3, 0), (1, 0), (0, 3), (0, 1)]
    side_blocks = [(2, 0), (3, 1), (1, 3), (3, 3), (1, 1)]
    far_blocks = [(2, 1), (2, 3), (0, 2), (3, 2), (1, 2), (2, 2)]
    first_hops(0)
    relay_hops(0, near_blocks)
    x_forward(1, 0)
    first_hops(1)
    x_forward(1, 1)
    relay_hops(0, side_blocks)
    relay_hops(1, near_blocks)
    x_forward(2, 0)
    relay_hops(0, far_blocks)
    own.wait()
    decay.wait()
    other_half(0)

    def nth(n):
        return (z + TEN + jnp.where(n % 2 == 1, -((n + 1) // 2), n // 2)) % TEN

    def many(part, lo_n, hi_n):
        def one(n, carry):
            project(nth(n), part)
            return carry
        lax.fori_loop(lo_n, hi_n, one, 0)

    def pairs(f, lo_n, hi_n):
        def one(n, carry):
            f(n)
            return carry
        lax.fori_loop(lo_n, hi_n, one, 0)

    def step(t, carry):
        when = lambda n: pl.when(t == n)

        @when(2)
        def _():
            x_forward(3, 1)

        @when(3)
        def _():
            for d in range(2):
                x_recv(d, 4, d).wait_recv()

        lo_n = jnp.where(t == 0, 0, 2 * t + 1)
        hi_n = jnp.minimum(2 * t + 3, TEN)
        many(0, lo_n, hi_n)
        many(1, lo_n, hi_n)

        @when(0)
        def _():
            x_forward(2, 1)
            relay_hops(1, side_blocks)

        keys_of(t)
        values_of(t)

        @when(0)
        def _():
            x_forward(3, 0)

        @when(1)
        def _():
            relay_hops(1, far_blocks)

        return carry

    lax.fori_loop(0, 4, step, 0)

    eye2 = (lax.broadcasted_iota(jnp.int32, (HD, 2 * HD), 0) == lax.broadcasted_iota(jnp.int32, (HD, 2 * HD), 1)).astype(bf16)
    zeros = jnp.zeros((HD, HD), f32)
    for h in range(HEADS):
        run[h] = eye2.astype(f32)

    def fold(c, carry):
        for h in range(HEADS):
            now = run[h]
            short = now.astype(bf16)
            pbs[c, h] = short
            run[h] = fin[c, h] * now - mm(ers[c, h], short) + jnp.concatenate([zeros, inj[c, h]], axis=1)
        return carry

    lax.fori_loop(0, TEN, fold, 0)
    for h in range(HEADS):
        pb[h] = run[h].astype(bf16)

    def unfold(c, carry):
        r = pl.ds(pl.multiple_of(c * CH, CH), CH)
        for h in range(HEADS):
            both = mm(rdr[c, h], pbs[c, h])
            rd[r, h * HD:(h + 1) * HD] = both[:, :HD].astype(bf16)
            lo[r, h * HD:(h + 1) * HD] = both[:, HD:] + loc[c, h]
        return carry

    def chain(later, earlier):
        p = mm(later[:, :HD], earlier)
        return (p + jnp.concatenate([zeros, later[:, HD:].astype(f32)], axis=1)).astype(bf16)

    chains = core == 0

    def up(h):
        return remote(pb.at[h], gc.at[me], upsem.at[0, h], upsem.at[1, me], column_dev(2 * h))

    def along(k):
        return remote(gx.at[cx], gx.at[cx], xsem.at[0, k], xsem.at[1, k], x_dev(k))

    def down(i):
        return remote(sb.at[i], sin.at[cy], downsem.at[0, i], downsem.at[1, cy], column_dev(i))

    def keeps(h):
        return chains & (cy == h)

    for h in range(HEADS):
        @pl.when(keeps(h))
        def _():
            gc[me] = pb[h]

        @pl.when(jnp.logical_not(keeps(h)))
        def _():
            up(h).start()

    other_half(1)
    many(2, 0, TEN)
    pairs(reads_of, 0, 4)

    @pl.when(chains)
    def _():
        for i in range(8):
            @pl.when(me != i)
            def _():
                remote(gc.at[i], gc.at[i], upsem.at[0, 0], upsem.at[1, i], column_dev(0)).wait_recv()
        two = [chain(gc[i + 1], gc[i]) for i in range(0, 8, 2)]
        four = [chain(two[1], two[0]), chain(two[3], two[2])]
        gx[cx] = chain(four[1], four[0])
        for k in (1, 2, 3):
            along(k).start()
        pre[0] = eye2
        pre[1] = gc[0]
        pre[2] = two[0]
        pre[3] = chain(gc[2], two[0])
        pre[4] = four[0]
        pre[5] = chain(gc[4], four[0])
        six = chain(two[2], four[0])
        pre[6] = six
        pre[7] = chain(gc[6], six)

    lax.fori_loop(0, TEN, unfold, 0)

    @pl.when(chains)
    def _():
        for k in (1, 2, 3):
            slot = gx.at[(cx + XN - k) % XN]
            remote(slot, slot, xsem.at[0, k], xsem.at[1, k], x_dev(k)).wait_recv()
        state = zeros
        begin[0] = state
        for k in range(XN - 1):
            state = mm(gx[k, :, :HD], state) + gx[k, :, HD:].astype(f32)
            begin[k + 1] = state
        state = begin[cx]
        for i in range(8):
            sb[i] = (mm(pre[i, :, :HD], state) + pre[i, :, HD:].astype(f32)).astype(bf16)

            @pl.when(me == i)
            def _():
                sin[cy] = sb[i]

            @pl.when(me != i)
            def _():
                down(i).start()

    for h in range(HEADS):
        @pl.when(jnp.logical_not(keeps(h)))
        def _():
            remote(sin.at[h], sin.at[h], downsem.at[0, 0], downsem.at[1, h], column_dev(0)).wait_recv()

    def attend(*chunks):
        rows = [pl.ds(pl.multiple_of(c * CH, CH), CH) for c in chunks]
        each = [(i, h) for i in range(len(chunks)) for h in range(HEADS)]
        att = [mm(rd[rows[i], h * HD:(h + 1) * HD], sin[h]) + lo[rows[i], h * HD:(h + 1) * HD] for i, h in each]
        for n, (i, h) in enumerate(each):
            scale = lax.rsqrt(jnp.mean(att[n] * att[n], axis=-1, keepdims=True) + 1e-5)
            nrm[chunks[i], :, h * HD:(h + 1) * HD] = (att[n] * scale * gain[...]).astype(bf16)

    def partials(*chunks):
        def tile(n, carry):
            at = pl.multiple_of(n * 384, 128)
            for d in range(2):
                part[d, :, pl.ds(at, 384)] = mm_nt(nrm[chunks[d]], wf[pl.ds(pl.multiple_of(d * HALF + at, 128), 384), OUT_AT:])
            return carry
        lax.fori_loop(0, HALF // 384, tile, 0)

    def send(d, t, u):
        rows = pl.ds(u * 64, 64)
        return remote(rsend.at[d, t, rows], rrecv.at[d, t, rows], rssem.at[d, t, u], rrsem.at[d, t, u], right if d == 0 else left)

    def ring(t, carry):
        ahead, behind = (z + 2 * TEN - 1 - t) % TEN, (z + 1 + t) % TEN

        @pl.when(t < 3)
        def _():
            attend(ahead, behind)

        @pl.when((t == 3) | (t == 7))
        def _():
            attend(ahead)

        partials(ahead, behind)
        for u in range(2):
            rows = pl.ds(u * 64, 64)
            for d in range(2):
                @pl.when(t > 0)
                def _():
                    send(d, t - 1, u).wait_recv()
                    part[d, rows] += rrecv[d, t - 1, rows].astype(f32)

                @pl.when(t < 7)
                def _():
                    rsend[d, t, rows] = part[d, rows].astype(bf16)
                    send(d, t, u).start()
        return carry

    lax.fori_loop(0, 8, ring, 0)
    for d in range(2):
        out[:, d * HALF:(d + 1) * HALF] = part[d].astype(bf16)

    @pl.when(s < SEQ - 1)
    def _():
        for copy in rims:
            copy.wait_send()

    pair.wait_send()
    for copy in sends:
        copy().wait_send()
    for d in range(2):
        for k in range(1, 5):
            for i in range(2):
                if k < 4 or i == d:
                    x_copy(d, k, i).wait_send()
    for h in range(HEADS):
        @pl.when(jnp.logical_not(keeps(h)))
        def _():
            up(h).wait_send()

    @pl.when(chains)
    def _():
        for k in (1, 2, 3):
            along(k).wait_send()
        for i in range(8):
            @pl.when(me != i)
            def _():
                down(i).wait_send()


    def drain(t, carry):
        for d in range(2):
            for u in range(2):
                send(d, t, u).wait_send()
        return carry

    lax.fori_loop(0, 7, drain, 0)


def layer(x, w_qkv, w_beta, w_out, gate, taps, gain):
    vm, dma = pltpu.VMEM, pltpu.SemaphoreType.DMA
    whole = pl.BlockSpec(memory_space=pltpu.VMEM)
    return pl.pallas_call(
        layer_body,
        in_specs=[whole] * 4 + [pl.BlockSpec(memory_space=pl.ANY), whole, whole],
        out_specs=whole,
        out_shape=jax.ShapeDtypeStruct((CH, COLS), bf16),
        scratch_shapes=[
            vm((TEN, CH, COLS), bf16),
            vm((COLS, COLS), bf16),
            vm((PIECE, COLS), bf16),
            vm((PIECE, COLS), bf16),
            vm((PAIR, COLS), f32),
            vm((16, QKV), bf16),
            vm((TEN * CH + 16, QKV), bf16),
            vm((TEN * CH, 128), f32),
            vm((TEN * CH, WIDTH), f32),
            vm((TEN, HEADS, 1, HD), f32),
            vm((TEN, HEADS, CH, HD), bf16),
            vm((TEN, HEADS, CH, HD), bf16),
            vm((TEN, HEADS, CH, HD), bf16),
            vm((TEN, HEADS, CH, HD), bf16),
            vm((TEN, HEADS, CH, HD), bf16),
            vm((TEN, HEADS, CH, HD), bf16),
            vm((TEN, HEADS, CH, HD), f32),
            vm((TEN, HEADS, HD, HD), bf16),
            vm((TEN, HEADS, HD, HD), f32),
            vm((TEN, HEADS, HD, 1), f32),
            vm((TEN, HEADS, HD, 2 * HD), bf16),
            vm((HEADS, HD, 2 * HD), f32),
            vm((HEADS, HD, 2 * HD), bf16),
            vm((TEN * CH, WIDTH), bf16),
            vm((TEN * CH, WIDTH), f32),
            vm((8, HD, 2 * HD), bf16),
            vm((8, HD, 2 * HD), bf16),
            vm((XN, HD, 2 * HD), bf16),
            vm((XN, HD, HD), f32),
            vm((8, HD, HD), bf16),
            vm((HEADS, HD, HD), bf16),
            vm((TEN, CH, WIDTH), bf16),
            vm((2, CH, HALF), f32),
            vm((2, 7, CH, HALF), bf16),
            vm((2, 7, CH, HALF), bf16),
            dma((2, 4, 2)), dma((2, 4, 2)), dma((2, 16)), dma((2, 16)), dma((2, 16)), dma((2, 16)),
            dma((4,)), dma((4,)), dma((2,)), dma((2, 8)), dma((2, 4)), dma((2, 8)), dma((2, 7, 2)), dma((2, 7, 2)),
        ],
        compiler_params=pltpu.CompilerParams(collective_id=0, has_side_effects=True, vmem_limit_bytes=62 << 20),
    )(x, w_qkv, w_beta, w_out, gate, taps, gain)


def per_device(x_rows, w_qkv, w_beta, conv_weight, log_decay, norm_gain, w_out):
    return layer(x_rows, w_qkv.transpose(1, 0, 2), w_beta.T, w_out.T, log_decay, conv_weight.reshape(4, QKV), norm_gain.reshape(1, HD))


def solution(mesh):
    in_specs = (
        P(("seq", "tensor"), None),
        P("seq", None, "tensor"),
        P("seq", "tensor"),
        P(None, None, "tensor"),
        P("seq", "tensor"),
        P(),
        P("tensor", "seq"),
    )
    return jax.shard_map(per_device, mesh=mesh, in_specs=in_specs, out_specs=P(("seq", "tensor"), None), check_vma=False)
```

```python
import functools
import jax
import jax.numpy as jnp
from jax import lax
from jax.experimental import pallas as pl
from jax.experimental.pallas import tpu as pltpu
from jax.sharding import PartitionSpec as P

f32, bf16 = jnp.float32, jnp.bfloat16
CH = 128
HD = 128


def mm(a, b):
    return jnp.dot(a.astype(bf16), b.astype(bf16), preferred_element_type=f32)


def mm_nt(a, b):
    return lax.dot_general(a.astype(bf16), b.astype(bf16), (((1,), (1,)), ((), ())), preferred_element_type=f32)


def mm_tn(a, b):
    return lax.dot_general(a.astype(bf16), b.astype(bf16), (((0,), (0,)), ((), ())), preferred_element_type=f32)


def triangle():
    row = lax.broadcasted_iota(jnp.int32, (CH, CH), 0)
    col = lax.broadcasted_iota(jnp.int32, (CH, CH), 1)
    return row, col


def short_conv(p, taps, at):
    p = p.astype(f32)
    y = taps[3:4, at:at + HD] * p[16:]
    for j in range(3):
        y = y + taps[j:j + 1, at:at + HD] * p[13 + j:13 + j + CH]
    return y * (0.5 + 0.5 * jnp.tanh(0.5 * y))


def unit(m):
    return m * lax.rsqrt(jnp.sum(m * m, axis=-1, keepdims=True) + 1e-6)


def unit_lower_inverse(mix):
    row, col = triangle()
    each = range(len(mix))
    near = (row // 16) == (col // 16)
    flat = []
    for h in each:
        m = jnp.where(near, mix[h].astype(f32), 0.0)
        total = m[0:16]
        for r in range(16, CH, 16):
            total = total + m[r:r + 16]
        flat.append(total.astype(bf16))
    flat = jnp.concatenate(flat, axis=0)
    row16 = lax.broadcasted_iota(jnp.int32, (16, CH), 0)
    col16 = lax.broadcasted_iota(jnp.int32, (16, CH), 1)
    small = [(row16 == col16 % 16).astype(f32) for h in each]
    for j in range(15):
        spread = mm(flat, near & ((row % 16) == j))
        small = [small[h] - spread[16 * h:16 * h + 16] * small[h][j:j + 1] for h in each]
    inv = [jnp.where(near, jnp.concatenate([small[h]] * (CH // 16), axis=0), 0.0) for h in each]
    zero = jnp.zeros((CH, CH), bf16)
    n = 16
    while n < CH:
        off = ((row // (2 * n)) == (col // (2 * n))) & ((row // n) % 2 == 1) & ((col // n) % 2 == 0)
        part = [jnp.where(off, mix[h], zero) for h in each]
        low = [inv[h].astype(bf16) for h in each]
        step = [mm(part[h], low[h]).astype(bf16) for h in each]
        inv = [inv[h] - mm(low[h], step[h]) for h in each]
        n *= 2
    return [inv[h].astype(bf16) for h in each]


def key_terms(keys, strength, decay):
    row, col = triangle()
    lower = (row >= col).astype(bf16)
    each = range(len(keys))
    k = [unit(m) for m in keys]
    ghi = [m.astype(bf16) for m in decay]
    glo = [(decay[h] - ghi[h].astype(f32)).astype(bf16) for h in each]
    cum = [mm(lower, ghi[h]) + mm(lower, glo[h]) for h in each]
    mid = [m[CH // 2 - 1:CH // 2] for m in cum]
    fin = [m[CH - 1:CH] for m in cum]
    rel = [cum[h] - mid[h] for h in each]
    k_up = [k[h] * jnp.exp(rel[h]) for h in each]
    k_down = [k[h] * jnp.exp(-rel[h]) for h in each]
    k_end = [(k_down[h] * jnp.exp(fin[h] - mid[h])).astype(bf16) for h in each]
    k_down = [m.astype(bf16) for m in k_down]
    mix = [mm_nt(k_up[h], k_down[h]) for h in each]
    mix = [jnp.where(row > col, strength[h] * mix[h], 0.0).astype(bf16) for h in each]
    inv = unit_lower_inverse(mix)
    emid = [jnp.exp(m) for m in mid]
    w = [mm(inv[h], strength[h] * (k_up[h] * emid[h])).astype(bf16) for h in each]
    erase = [mm_tn(k_end[h], w[h]).astype(bf16) for h in each]
    final = [jnp.sum(jnp.where(row == col, jnp.exp(fin[h]), 0.0), axis=1, keepdims=True) for h in each]
    return rel, emid, k_down, k_end, inv, w, erase, final


def value_terms(values, strength, k_end, inv):
    each = range(len(values))
    u = [mm(inv[h], strength[h] * values[h]).astype(bf16) for h in each]
    inject = [mm_tn(k_end[h], u[h]) for h in each]
    return u, inject


def read_terms(query, rel, emid, k_down, w, u):
    row, col = triangle()
    each = range(len(query))
    q = [unit(query[h]) * jnp.exp(rel[h]) for h in each]
    score = [jnp.where(row >= col, mm_nt(q[h], k_down[h]), 0.0).astype(bf16) for h in each]
    sw = [mm(score[h], jnp.concatenate([w[h], u[h]], axis=1)) for h in each]
    reader = [(q[h] * emid[h] - sw[h][:, :HD]).astype(bf16) for h in each]
    local = [sw[h][:, HD:] for h in each]
    return reader, local


MESH = pl.DeviceIdType.MESH
XN, YN = 4, 4
SEQ, TEN = 32, 8
PIECE = 72
PAIR = 2 * PIECE
COLS = 2304
HALF = COLS // 2
HEADS = 4
WIDTH = HEADS * HD
QKV = 1536
BETA_AT = 512
V_AT = 768
Q_AT = 1280
OUT_AT = 1792


def place():
    s, z = lax.axis_index("seq"), lax.axis_index("tensor")
    core, chip = s % 2, s // 2
    return s, z, core, chip // YN, chip % YN


def remote(src, dst, ssem, rsem, to):
    copy = pltpu.make_async_remote_copy(src_ref=src, dst_ref=dst, send_sem=ssem, recv_sem=rsem, device_id=to, device_id_type=MESH)
    return copy


def greet(peers):
    barrier = pltpu.get_barrier_semaphore()
    for peer in peers:
        pl.semaphore_signal(barrier, inc=1, device_id=peer, device_id_type=MESH)
    pl.semaphore_wait(barrier, len(peers))


def layer_body(x, w_qkv, w_beta, w_out, gate_in, taps, gain, out,
               xg, wf, w, sib, blk, rim, proj, logit, gate, emid, kdn, ken, inv, wk, uv, rdr, loc, ers, inj, fin, pbs, run, pb, rd, lo,
               gc, pre, gx, begin, sb, sin, nrm, part, rsend, rrecv,
               xs, xr, ws, wr, ss, sr, ps, pr, ls, upsem, xsem, downsem, rssem, rrsem):
    s, z, core, cx, cy = place()
    a = jnp.where(core == 0, cx, cy)
    b = jnp.where(core == 0, cy, cx)

    def chip_of(da, db):
        ra, rb = (a + da) % 4, (b + db) % 4
        return jnp.where(core == 0, ra * YN + rb, rb * YN + ra)

    def dev_of(da, db):
        return (chip_of(da, db) * 2 + core, z)

    other = (s + 1 - 2 * core, z)
    right, left = (s, (z + 1) % TEN), (s, (z + TEN - 1) % TEN)
    after, before = ((s + 1) % SEQ, z), ((s + SEQ - 1) % SEQ, z)
    def column_dev(i):
        return ((cx * YN + i // 2) * 2 + i % 2, z)

    def x_dev(k):
        return ((((cx + k) % XN) * YN + cy) * 2 + core, z)

    me = cy * 2 + core
    greet([right, left, after, before] + [x_dev(k) for k in (1, 2, 3)] + [column_dev((me + k) % 8) for k in range(1, 8)])

    def x_copy(d, k, i):
        c, r = (z + (TEN - k + 1 if d == 0 else k - 1)) % TEN, pl.ds(64 * i, 64)
        here = xg.at[c, r]
        return remote(x.at[r] if k == 1 else here, here, xs.at[d, k - 1, i], xr.at[d, k - 1, i], right if d == 0 else left)

    def x_recv(d, k, i):
        here = xg.at[(z + (TEN - k if d == 0 else k)) % TEN, pl.ds(64 * i, 64)]
        return remote(here, here, xs.at[d, k - 1, i], xr.at[d, k - 1, i], right if d == 0 else left)

    w[:, :BETA_AT] = w_qkv[1]
    spread = (lax.broadcasted_iota(jnp.int32, (HEADS, V_AT - BETA_AT), 0) == lax.broadcasted_iota(jnp.int32, (HEADS, V_AT - BETA_AT), 1))
    w[:, BETA_AT:V_AT] = mm_tn(w_beta[...], spread).astype(bf16)
    w[:, V_AT:Q_AT] = w_qkv[2]
    w[:, Q_AT:OUT_AT] = w_qkv[0]
    w[:, OUT_AT:] = w_out[...]
    pair = remote(w, sib, ps.at[0], pr.at[0], other)
    pair.start()
    for i in range(2):
        for d in range(2):
            x_copy(d, 1, i ^ d).start()

    own = pltpu.make_async_copy(x, xg.at[z], ls.at[0])
    own.start()
    decay = pltpu.make_async_copy(gate_in, gate, ls.at[1])
    decay.start()
    pair.wait_recv()
    mine = w[...].astype(f32)
    theirs = sib[...].astype(f32)
    blk[0:PIECE] = jnp.where(core == 0, mine, theirs)
    blk[PIECE:PAIR] = jnp.where(core == 0, theirs, mine)
    here = pl.multiple_of(chip_of(0, 0) * PAIR, 16)
    wf[pl.ds(here, PAIR)] = blk[...].astype(bf16)

    def w_ref(g, da, db, who=core):
        full, first, n = ((wf, 0, Q_AT // 2), (wf, Q_AT, (COLS - Q_AT) // 2))[g]
        rows = pl.ds(pl.multiple_of(chip_of(da, db) * PAIR, 16), PAIR)
        return full.at[rows, pl.ds(pl.multiple_of(first + who * n, 128), n)]

    sends = []
    used = [0] * 2

    def w_send(g, da, db, ta, tb):
        ra, rb = (da - ta) % 4, (db - tb) % 4
        n = used[g]
        used[g] += 1

        def copy():
            ref = w_ref(g, da, db)
            return remote(ref, ref, ws.at[g, n], wr.at[g, ra * 4 + rb], dev_of(ta, tb))

        copy().start()
        sends.append(copy)

    def w_wait(g, da, db):
        ref = w_ref(g, da, db)
        remote(ref, ref, ws.at[g, 0], wr.at[g, da * 4 + db], other).wait_recv()

    def across(g, da, db):
        def copy():
            ref = w_ref(g, da, db)
            return remote(ref, ref, ss.at[g, da * 4 + db], sr.at[g, da * 4 + db], other)

        copy().start()
        sends.append(copy)

    def hop_b(g, da):
        w_send(g, da, 0, 0, 1)
        w_send(g, da, 0, 0, 3)

    def first_hops(g):
        w_send(g, 0, 0, 1, 0)
        w_send(g, 0, 0, 3, 0)
        hop_b(g, 0)

    def relay_hops(g, blocks):
        for da, db in blocks:
            w_wait(g, da, db)
            if (da, db) == (3, 0):
                w_send(g, da, db, 1, 0)
            if db == 0:
                hop_b(g, da)
            if (db == 3 and da < 2) or (db == 1 and da > 1):
                w_send(g, da, db, 0, 1 if db == 3 else 3)
            across(g, da, db)

    def other_half(g):
        for i in range(1, 16):
            ref = w_ref(g, i % 4, i // 4, 1 - core)
            remote(ref, ref, ss.at[g, i], sr.at[g, i], other).wait_recv()

    def x_forward(k, i):
        for d in range(2):
            x_recv(d, k, i ^ d).wait_recv()
            if k < 3 or i == 0:
                x_copy(d, k + 1, i ^ d).start()

    rims = []
    for n in range(3):
        cols = pl.ds(n * WIDTH, WIDTH)
        rims.append(remote(proj.at[pl.ds(TEN * CH, 16), cols], rim.at[:, cols], ps.at[1 + n], pr.at[1 + n], after))

    @pl.when(s == 0)
    def _():
        proj[0:16] = jnp.zeros((16, QKV), bf16)

    def project(c, part):
        r = pl.multiple_of(16 + c * CH, 16)
        if part == 0:
            acc = jnp.dot(xg[c], wf[:, :Q_AT], preferred_element_type=f32)
            proj[pl.ds(r, CH), :WIDTH] = acc[:, :WIDTH].astype(bf16)
            proj[pl.ds(r, CH), WIDTH:2 * WIDTH] = acc[:, V_AT:].astype(bf16)
            logit[pl.ds(pl.multiple_of(c * CH, CH), CH)] = acc[:, BETA_AT:BETA_AT + 128]
        else:
            acc = jnp.dot(xg[c], wf[:, Q_AT:OUT_AT], preferred_element_type=f32)
            proj[pl.ds(r, CH), 2 * WIDTH:] = acc.astype(bf16)

        @pl.when((c == TEN - 1) & (s < SEQ - 1))
        def _():
            for n in ((0, 1) if part == 0 else (2,)):
                rims[n].start()

    def pair_of(k):
        chunks = [(z + TEN - k) % TEN, (z + k + 1) % TEN]
        return chunks, [pl.multiple_of(c * CH, CH) for c in chunks], [(i, h) for i in range(2) for h in range(HEADS)]

    def rim_in(chunks, part):
        @pl.when((s > 0) & ((chunks[0] == 0) | (chunks[1] == 0)))
        def _():
            rims[part].wait_recv()
            proj[0:16, part * WIDTH:(part + 1) * WIDTH] = rim[:, part * WIDTH:(part + 1) * WIDTH]

    def strengths(at):
        b = [1.0 / (1.0 + jnp.exp(-logit[pl.ds(at[i], CH)])) for i in range(2)]
        return [b[i][:, h:h + 1] for i in range(2) for h in range(HEADS)]

    def conv(at, i, h, part):
        col, tap = part * WIDTH + h * HD, ((1, 2, 0)[part]) * WIDTH + h * HD
        return short_conv(proj[pl.ds(at[i], CH + 16), col:col + HD], taps, tap)

    def put(chunks, each, refs, got):
        for n, (i, h) in enumerate(each):
            for ref, value in zip(refs, got):
                ref[chunks[i], h] = value[n]

    def take(chunks, each, *refs):
        return [[ref[chunks[i], h] for i, h in each] for ref in refs]

    def decays(at, each):
        return [gate[pl.ds(at[i], CH), h * HD:(h + 1) * HD] for i, h in each]

    def keys_of(k):
        chunks, at, each = pair_of(k)
        rim_in(chunks, 0)
        got = key_terms([conv(at, i, h, 0) for i, h in each], strengths(at), decays(at, each))
        for n, (i, h) in enumerate(each):
            gate[pl.ds(at[i], CH), h * HD:(h + 1) * HD] = got[0][n]
        put(chunks, each, (emid, kdn, ken, inv, wk, ers, fin), got[1:])

    def values_of(k):
        chunks, at, each = pair_of(k)
        rim_in(chunks, 1)
        got = value_terms([conv(at, i, h, 1) for i, h in each], strengths(at), *take(chunks, each, ken, inv))
        put(chunks, each, (uv, inj), got)

    def reads_of(k):
        chunks, at, each = pair_of(k)
        rim_in(chunks, 2)
        got = read_terms([conv(at, i, h, 2) for i, h in each], decays(at, each), *take(chunks, each, emid, kdn, wk, uv))
        put(chunks, each, (rdr, loc), got)

    near_blocks = [(3, 0), (1, 0), (0, 3), (0, 1)]
    side_blocks = [(2, 0), (3, 1), (1, 3), (3, 3), (1, 1)]
    far_blocks = [(2, 1), (2, 3), (0, 2), (3, 2), (1, 2), (2, 2)]
    first_hops(0)
    relay_hops(0, near_blocks)
    x_forward(1, 0)
    first_hops(1)
    x_forward(1, 1)
    relay_hops(0, side_blocks)
    relay_hops(1, near_blocks)
    x_forward(2, 0)
    relay_hops(0, far_blocks)
    own.wait()
    decay.wait()
    other_half(0)

    def nth(n):
        return (z + TEN + jnp.where(n % 2 == 1, -((n + 1) // 2), n // 2)) % TEN

    def many(part, lo_n, hi_n):
        def one(n, carry):
            project(nth(n), part)
            return carry
        lax.fori_loop(lo_n, hi_n, one, 0)

    def pairs(f, lo_n, hi_n):
        def one(n, carry):
            f(n)
            return carry
        lax.fori_loop(lo_n, hi_n, one, 0)

    def step(t, carry):
        when = lambda n: pl.when(t == n)

        @when(2)
        def _():
            x_forward(3, 1)

        @when(3)
        def _():
            for d in range(2):
                x_recv(d, 4, d).wait_recv()

        lo_n = jnp.where(t == 0, 0, 2 * t + 1)
        hi_n = jnp.minimum(2 * t + 3, TEN)
        many(0, lo_n, hi_n)

        @when(0)
        def _():
            x_forward(2, 1)
            relay_hops(1, side_blocks)

        keys_of(t)
        values_of(t)

        @when(0)
        def _():
            x_forward(3, 0)

        @when(1)
        def _():
            relay_hops(1, far_blocks)

        return carry

    lax.fori_loop(0, 4, step, 0)

    eye2 = (lax.broadcasted_iota(jnp.int32, (HD, 2 * HD), 0) == lax.broadcasted_iota(jnp.int32, (HD, 2 * HD), 1)).astype(bf16)
    zeros = jnp.zeros((HD, HD), f32)
    for h in range(HEADS):
        run[h] = eye2.astype(f32)

    def fold(c, carry):
        for h in range(HEADS):
            now = run[h]
            short = now.astype(bf16)
            pbs[c, h] = short
            run[h] = fin[c, h] * now - mm(ers[c, h], short) + jnp.concatenate([zeros, inj[c, h]], axis=1)
        return carry

    lax.fori_loop(0, TEN, fold, 0)
    for h in range(HEADS):
        pb[h] = run[h].astype(bf16)

    def unfold(c, carry):
        r = pl.ds(pl.multiple_of(c * CH, CH), CH)
        for h in range(HEADS):
            both = mm(rdr[c, h], pbs[c, h])
            rd[r, h * HD:(h + 1) * HD] = both[:, :HD].astype(bf16)
            lo[r, h * HD:(h + 1) * HD] = both[:, HD:] + loc[c, h]
        return carry

    def chain(later, earlier):
        p = mm(later[:, :HD], earlier)
        return (p + jnp.concatenate([zeros, later[:, HD:].astype(f32)], axis=1)).astype(bf16)

    chains = core == 0

    def up(h):
        return remote(pb.at[h], gc.at[me], upsem.at[0, h], upsem.at[1, me], column_dev(2 * h))

    def along(k):
        return remote(gx.at[cx], gx.at[cx], xsem.at[0, k], xsem.at[1, k], x_dev(k))

    def down(i):
        return remote(sb.at[i], sin.at[cy], downsem.at[0, i], downsem.at[1, cy], column_dev(i))

    def keeps(h):
        return chains & (cy == h)

    for h in range(HEADS):
        @pl.when(keeps(h))
        def _():
            gc[me] = pb[h]

        @pl.when(jnp.logical_not(keeps(h)))
        def _():
            up(h).start()

    other_half(1)
    many(2, 0, TEN)
    pairs(reads_of, 0, 4)

    @pl.when(chains)
    def _():
        for i in range(8):
            @pl.when(me != i)
            def _():
                remote(gc.at[i], gc.at[i], upsem.at[0, 0], upsem.at[1, i], column_dev(0)).wait_recv()
        two = [chain(gc[i + 1], gc[i]) for i in range(0, 8, 2)]
        four = [chain(two[1], two[0]), chain(two[3], two[2])]
        gx[cx] = chain(four[1], four[0])
        for k in (1, 2, 3):
            along(k).start()
        pre[0] = eye2
        pre[1] = gc[0]
        pre[2] = two[0]
        pre[3] = chain(gc[2], two[0])
        pre[4] = four[0]
        pre[5] = chain(gc[4], four[0])
        six = chain(two[2], four[0])
        pre[6] = six
        pre[7] = chain(gc[6], six)

    lax.fori_loop(0, TEN, unfold, 0)

    @pl.when(chains)
    def _():
        for k in (1, 2, 3):
            slot = gx.at[(cx + XN - k) % XN]
            remote(slot, slot, xsem.at[0, k], xsem.at[1, k], x_dev(k)).wait_recv()
        state = zeros
        begin[0] = state
        for k in range(XN - 1):
            state = mm(gx[k, :, :HD], state) + gx[k, :, HD:].astype(f32)
            begin[k + 1] = state
        state = begin[cx]
        for i in range(8):
            sb[i] = (mm(pre[i, :, :HD], state) + pre[i, :, HD:].astype(f32)).astype(bf16)

            @pl.when(me == i)
            def _():
                sin[cy] = sb[i]

            @pl.when(me != i)
            def _():
                down(i).start()

    for h in range(HEADS):
        @pl.when(jnp.logical_not(keeps(h)))
        def _():
            remote(sin.at[h], sin.at[h], downsem.at[0, 0], downsem.at[1, h], column_dev(0)).wait_recv()

    def attend(*chunks):
        rows = [pl.ds(pl.multiple_of(c * CH, CH), CH) for c in chunks]
        each = [(i, h) for i in range(len(chunks)) for h in range(HEADS)]
        att = [mm(rd[rows[i], h * HD:(h + 1) * HD], sin[h]) + lo[rows[i], h * HD:(h + 1) * HD] for i, h in each]
        for n, (i, h) in enumerate(each):
            scale = lax.rsqrt(jnp.mean(att[n] * att[n], axis=-1, keepdims=True) + 1e-5)
            nrm[chunks[i], :, h * HD:(h + 1) * HD] = (att[n] * scale * gain[...]).astype(bf16)

    def partials(*chunks):
        def tile(n, carry):
            at = pl.multiple_of(n * 384, 128)
            for d in range(2):
                part[d, :, pl.ds(at, 384)] = mm_nt(nrm[chunks[d]], wf[pl.ds(pl.multiple_of(d * HALF + at, 128), 384), OUT_AT:])
            return carry
        lax.fori_loop(0, HALF // 384, tile, 0)

    def send(d, t, u):
        rows = pl.ds(u * 64, 64)
        return remote(rsend.at[d, t, rows], rrecv.at[d, t, rows], rssem.at[d, t, u], rrsem.at[d, t, u], right if d == 0 else left)

    def ring(t, carry):
        ahead, behind = (z + 2 * TEN - 1 - t) % TEN, (z + 1 + t) % TEN

        @pl.when(t < 3)
        def _():
            attend(ahead, behind)

        @pl.when((t == 3) | (t == 7))
        def _():
            attend(ahead)

        partials(ahead, behind)
        for u in range(2):
            rows = pl.ds(u * 64, 64)
            for d in range(2):
                @pl.when(t > 0)
                def _():
                    send(d, t - 1, u).wait_recv()
                    part[d, rows] += rrecv[d, t - 1, rows].astype(f32)

                @pl.when(t < 7)
                def _():
                    rsend[d, t, rows] = part[d, rows].astype(bf16)
                    send(d, t, u).start()
        return carry

    lax.fori_loop(0, 8, ring, 0)
    for d in range(2):
        out[:, d * HALF:(d + 1) * HALF] = part[d].astype(bf16)

    @pl.when(s < SEQ - 1)
    def _():
        for copy in rims:
            copy.wait_send()

    pair.wait_send()
    for copy in sends:
        copy().wait_send()
    for d in range(2):
        for k in range(1, 5):
            for i in range(2):
                if k < 4 or i == d:
                    x_copy(d, k, i).wait_send()
    for h in range(HEADS):
        @pl.when(jnp.logical_not(keeps(h)))
        def _():
            up(h).wait_send()

    @pl.when(chains)
    def _():
        for k in (1, 2, 3):
            along(k).wait_send()
        for i in range(8):
            @pl.when(me != i)
            def _():
                down(i).wait_send()


    def drain(t, carry):
        for d in range(2):
            for u in range(2):
                send(d, t, u).wait_send()
        return carry

    lax.fori_loop(0, 7, drain, 0)


def layer(x, w_qkv, w_beta, w_out, gate, taps, gain):
    vm, dma = pltpu.VMEM, pltpu.SemaphoreType.DMA
    whole = pl.BlockSpec(memory_space=pltpu.VMEM)
    return pl.pallas_call(
        layer_body,
        in_specs=[whole] * 4 + [pl.BlockSpec(memory_space=pl.ANY), whole, whole],
        out_specs=whole,
        out_shape=jax.ShapeDtypeStruct((CH, COLS), bf16),
        scratch_shapes=[
            vm((TEN, CH, COLS), bf16),
            vm((COLS, COLS), bf16),
            vm((PIECE, COLS), bf16),
            vm((PIECE, COLS), bf16),
            vm((PAIR, COLS), f32),
            vm((16, QKV), bf16),
            vm((TEN * CH + 16, QKV), bf16),
            vm((TEN * CH, 128), f32),
            vm((TEN * CH, WIDTH), f32),
            vm((TEN, HEADS, 1, HD), f32),
            vm((TEN, HEADS, CH, HD), bf16),
            vm((TEN, HEADS, CH, HD), bf16),
            vm((TEN, HEADS, CH, HD), bf16),
            vm((TEN, HEADS, CH, HD), bf16),
            vm((TEN, HEADS, CH, HD), bf16),
            vm((TEN, HEADS, CH, HD), bf16),
            vm((TEN, HEADS, CH, HD), f32),
            vm((TEN, HEADS, HD, HD), bf16),
            vm((TEN, HEADS, HD, HD), f32),
            vm((TEN, HEADS, HD, 1), f32),
            vm((TEN, HEADS, HD, 2 * HD), bf16),
            vm((HEADS, HD, 2 * HD), f32),
            vm((HEADS, HD, 2 * HD), bf16),
            vm((TEN * CH, WIDTH), bf16),
            vm((TEN * CH, WIDTH), f32),
            vm((8, HD, 2 * HD), bf16),
            vm((8, HD, 2 * HD), bf16),
            vm((XN, HD, 2 * HD), bf16),
            vm((XN, HD, HD), f32),
            vm((8, HD, HD), bf16),
            vm((HEADS, HD, HD), bf16),
            vm((TEN, CH, WIDTH), bf16),
            vm((2, CH, HALF), f32),
            vm((2, 7, CH, HALF), bf16),
            vm((2, 7, CH, HALF), bf16),
            dma((2, 4, 2)), dma((2, 4, 2)), dma((2, 16)), dma((2, 16)), dma((2, 16)), dma((2, 16)),
            dma((4,)), dma((4,)), dma((2,)), dma((2, 8)), dma((2, 4)), dma((2, 8)), dma((2, 7, 2)), dma((2, 7, 2)),
        ],
        compiler_params=pltpu.CompilerParams(collective_id=0, has_side_effects=True, vmem_limit_bytes=62 << 20),
    )(x, w_qkv, w_beta, w_out, gate, taps, gain)


def per_device(x_rows, w_qkv, w_beta, conv_weight, log_decay, norm_gain, w_out):
    return layer(x_rows, w_qkv.transpose(1, 0, 2), w_beta.T, w_out.T, log_decay, conv_weight.reshape(4, QKV), norm_gain.reshape(1, HD))


def solution(mesh):
    in_specs = (
        P(("seq", "tensor"), None),
        P("seq", None, "tensor"),
        P("seq", "tensor"),
        P(None, None, "tensor"),
        P("seq", "tensor"),
        P(),
        P("tensor", "seq"),
    )
    return jax.shard_map(per_device, mesh=mesh, in_specs=in_specs, out_specs=P(("seq", "tensor"), None), check_vma=False)
```
